128 devices in a mesh: ctx: 32 (over x_lo, y, z), fsdp: 4 (over x_hi, core).
Axes of the slice: x: 4 (x_hi: 2, x_lo: 2; x = x_hi * 2 + x_lo), y: 4, z: 4, core: 2. Of those that a mesh axis runs over, the one named last changes fastest.
Arguments:
- tokens: bfloat16 [32, 4, 128, 1024], P('ctx', 'fsdp'), may hold values from -6 to 6
- block_order: int32 [32], replicated, may hold values from 0 to 31, each once
- weight_qkv: bfloat16 [1024, 3072], P('fsdp'), may hold values from -0.1875 to 0.1875
- bias_qkv: bfloat16 [3072], P('fsdp'), may hold values from -2 to 2
- weight_dense: bfloat16 [1024, 1024], P('fsdp'), may hold values from -3 to 3
- bias_dense: bfloat16 [1024], P('fsdp'), may hold values from -3 to 3
- weight_up: bfloat16 [1024, 4096], P('fsdp'), may hold values from -0.1875 to 0.1875
- bias_up: bfloat16 [4096], P('fsdp'), may hold values from -3 to 3
- weight_down: bfloat16 [1024, 4096], P('fsdp'), may hold values from -0.09375 to 0.09375
- bias_down: bfloat16 [1024], P('fsdp'), may hold values from -3 to 3
- gain_one: bfloat16 [1024], P('fsdp'), may hold values from 0.5 to 1.5
- shift_one: bfloat16 [1024], P('fsdp'), may hold values from -2 to 2
- gain_two: bfloat16 [1024], P('fsdp'), may hold values from 0.5 to 1.5
- shift_two: bfloat16 [1024], P('fsdp'), may hold values from -2 to 2
- cotangent: bfloat16 [32, 4, 128, 1024], P('ctx', 'fsdp'), may hold values from -6 to 6
Outputs:
- out_block: bfloat16 [32, 4, 128, 1024], P('ctx', 'fsdp')
- grad_tokens: bfloat16 [32, 4, 128, 1024], P('ctx', 'fsdp')
- grad_weight_qkv: float32 [1024, 3072], P('fsdp')
- grad_bias_qkv: float32 [3072], P('fsdp')
- grad_weight_dense: float32 [1024, 1024], P('fsdp')
- grad_bias_dense: float32 [1024], P('fsdp')
- grad_weight_up: float32 [1024, 4096], P('fsdp')
- grad_bias_up: float32 [4096], P('fsdp')
- grad_weight_down: float32 [1024, 4096], P('fsdp')
- grad_bias_down: float32 [1024], P('fsdp')
- grad_gain_one: float32 [1024], P('fsdp')
- grad_shift_one: float32 [1024], P('fsdp')
- grad_gain_two: float32 [1024], P('fsdp')
- grad_shift_two: float32 [1024], P('fsdp')
The draws below stay inside these ranges and needn't reach their ends.
Inputs may be any that keep to these rules, and one draw needn't show every extreme that they name: block_order names each of 0 to 31 once.
All inputs are finite; a program needn't handle non-finite values.
Results may differ from the reference program's by a relative error of at most 0.025.
Values may be sent and summed in bfloat16 or wider, within the bound.
No kernel may reach another device: no remote copies, remote signals or barrier semaphores. Data moves between devices by JAX's collectives and lax.ppermute only.
A program may use at most 192 MiB of HBM per device.

```python
import jax
import jax.numpy as jnp
from jax import lax

D = 1024
HEADS = 16
HEAD_DIM = 64
FF = 4096
ROT_DIMS = 16
TOK_DEV = 128
BLOCKS = 32
SEQS = 4
N_CTX = 32


def shard_levels(stream_key, dims, pieces, smallest, high):
    factor_of, own = 1.0, jax.random.fold_in(stream_key, 6)
    for axis_at, shards_of in pieces:
        heights = jnp.exp(jax.random.uniform(jax.random.fold_in(own, axis_at), (shards_of,), jnp.float32, smallest / len(pieces), high / len(pieces)))
        factor_of = factor_of * jnp.repeat(heights, dims[axis_at] // shards_of).reshape([-1 if axis == axis_at else 1 for axis in range(len(dims))])
    return factor_of


def noise(own_key, shape, scale, reach, split=(), held_as=jnp.bfloat16):
    array = scale * jax.random.normal(own_key, shape, jnp.float32)
    if split:
        array = array * shard_levels(own_key, shape, split, -0.22, 0.18)
    return jnp.clip(array, -reach, reach).astype(held_as)


def setup_inputs(seed: int = 0) -> dict:
    streams_of = jax.random.split(jax.random.key(seed), 16)
    tokens = noise(streams_of[0], (BLOCKS, SEQS, TOK_DEV, D), 1.0, 6.0, ((0, 32), (1, 4)))
    block_order = jax.random.permutation(streams_of[1], BLOCKS).astype(jnp.int32)
    weight_qkv = noise(streams_of[2], (D, 3 * D), D ** -0.5, 0.1875, ((0, 4),))
    bias_qkv = noise(streams_of[3], (3 * D,), 0.3, 2.0, ((0, 4),))
    weight_dense = noise(streams_of[4], (D, D), (max(1, D // 256)) ** -0.5, 3.0, ((0, 4),))
    bias_dense = noise(streams_of[5], (D,), 0.5, 3.0, ((0, 4),))
    weight_up = noise(streams_of[6], (D, FF), D ** -0.5, 0.1875, ((0, 4),))
    bias_up = noise(streams_of[7], (FF,), 0.5, 3.0, ((0, 4),))
    weight_down = noise(streams_of[8], (D, FF), FF ** -0.5, 0.09375, ((0, 4),))
    bias_down = noise(streams_of[9], (D,), 0.5, 3.0, ((0, 4),))
    gain_one = jnp.clip(1.0 + 0.1 * jax.random.normal(streams_of[10], (D,), jnp.float32), 0.5, 1.5).astype(jnp.bfloat16)
    shift_one = noise(streams_of[11], (D,), 0.3, 2.0, ((0, 4),))
    gain_two = jnp.clip(1.0 + 0.1 * jax.random.normal(streams_of[12], (D,), jnp.float32), 0.5, 1.5).astype(jnp.bfloat16)
    shift_two = noise(streams_of[13], (D,), 0.3, 2.0, ((0, 4),))
    cotangent = noise(streams_of[14], (BLOCKS, SEQS, TOK_DEV, D), 1.0, 6.0, ((0, 32), (1, 4)))
    return {"tokens": tokens, "block_order": block_order, "weight_qkv": weight_qkv, "bias_qkv": bias_qkv, "weight_dense": weight_dense, "bias_dense": bias_dense, "weight_up": weight_up, "bias_up": bias_up, "weight_down": weight_down, "bias_down": bias_down, "gain_one": gain_one, "shift_one": shift_one, "gain_two": gain_two, "shift_two": shift_two, "cotangent": cotangent}


EPSILON = 1e-05
NEGATIVE = -1e+30
PRECISE = lax.Precision.HIGHEST

@jax.custom_vjp
def low(v):
    return lax.optimization_barrier(v.astype(jnp.bfloat16)).astype(jnp.float32)

@jax.custom_vjp
def low_back(v):
    return v

def low_keep(v):
    return (low(v), None)

def low_pass(kept, grad):
    return (grad,)

def back_keep(v):
    return (v, None)

def back_low(kept, grad):
    return (low(grad),)
low.defvjp(low_keep, low_pass)
low_back.defvjp(back_keep, back_low)

def layer_norm(inputs, scaling, offsets):
    centre = inputs - lax.optimization_barrier(jnp.mean(inputs, axis=-1, keepdims=True))
    spread = lax.optimization_barrier(jnp.mean(centre * centre, axis=-1, keepdims=True))
    return centre * lax.rsqrt(spread + EPSILON) * scaling + offsets

def rotary(inputs, cosines, sine_vals):
    halfway = cosines.shape[-1] // 2
    turned = inputs[..., :2 * halfway]
    swapped = jnp.concatenate([-turned[..., halfway:], turned[..., :halfway]], axis=-1)
    turned = turned * cosines + swapped * sine_vals
    return jnp.concatenate([turned, inputs[..., 2 * halfway:]], axis=-1)

def angles(places):
    halfway = ROT_DIMS // 2
    inverse = 10000.0 ** (-2.0 * jnp.arange(halfway).astype(places.dtype) / ROT_DIMS)
    phases = places[:, None] * inverse[None, :]
    phases = jnp.concatenate([phases, phases], axis=-1)
    return (jnp.cos(phases)[:, None, :], jnp.sin(phases)[:, None, :])

def attend(queries, key_rows, values, positions):
    length = queries.shape[0]
    block_size = min(512, length)
    block_count = length // block_size
    score_scale = HEAD_DIM ** (-0.5)

    def one_block(operands):
        query_rows, places = operands
        scores = low_back(jnp.einsum('qhd,khd->qhk', query_rows, key_rows, precision=PRECISE) * score_scale)
        allowed = (positions[None, :] <= places[:, None])[:, None, :]
        scores = jnp.where(allowed, scores, NEGATIVE)
        row_max = lax.optimization_barrier(jnp.max(scores, axis=-1, keepdims=True))
        weights = jnp.exp(scores - row_max)
        probability = low(weights / lax.optimization_barrier(jnp.sum(weights, axis=-1, keepdims=True)))
        mixture = jnp.einsum('qhk,khd->qhd', probability, values, precision=PRECISE)
        return mixture.reshape(block_size, HEADS * HEAD_DIM)
    stacked = lax.map(jax.checkpoint(one_block), (queries.reshape(block_count, block_size, HEADS, HEAD_DIM), positions.reshape(block_count, block_size)))
    return stacked.reshape(length, HEADS * HEAD_DIM)

def sequence_forward(sequence_in, positions, params):
    weight_qkv, bias_qkv, weight_dense, bias_dense, weight_up, bias_up, weight_down, bias_down, gain_one, shift_one, gain_two, shift_two = params
    length = sequence_in.shape[0]
    normed_one = low(layer_norm(sequence_in, gain_one, shift_one))
    projected = low_back(jnp.dot(normed_one, weight_qkv, precision=PRECISE) + bias_qkv)
    projected = projected.reshape(length, 3, HEADS, HEAD_DIM)
    cosines, sine_vals = angles(positions.astype(sequence_in.dtype))
    queries = low(rotary(projected[:, 0], cosines, sine_vals))
    key_rows = low(rotary(projected[:, 1], cosines, sine_vals))
    values = low(projected[:, 2])
    attended = low(low_back(attend(queries, key_rows, values, positions)))
    normed_two = low(layer_norm(sequence_in, gain_two, shift_two))
    upward = low_back(jnp.dot(normed_two, weight_up, precision=PRECISE) + bias_up)
    activated = low(jax.nn.gelu(upward, approximate=False))
    branch_att = jnp.dot(attended, weight_dense, precision=PRECISE) + bias_dense
    branch_mlp = jnp.dot(activated, weight_down.T, precision=PRECISE) + bias_down
    return sequence_in + branch_att + branch_mlp

def reference(tokens, block_order, weight_qkv, bias_qkv, weight_dense, bias_dense, weight_up, bias_up, weight_down, bias_down, gain_one, shift_one, gain_two, shift_two, cotangent):
    params = tuple((matrix.astype(jnp.float32) for matrix in (weight_qkv, bias_qkv, weight_dense, bias_dense, weight_up, bias_up, weight_down, bias_down, gain_one, shift_one, gain_two, shift_two)))
    positions = (block_order[:, None].astype(jnp.int32) * TOK_DEV + jnp.arange(TOK_DEV, dtype=jnp.int32)[None, :]).reshape(N_CTX * TOK_DEV).astype(jnp.int32)
    sequences = jnp.swapaxes(tokens.astype(jnp.float32), 0, 1).reshape(SEQS, N_CTX * TOK_DEV, D)
    cotangents = jnp.swapaxes(cotangent.astype(jnp.float32), 0, 1).reshape(SEQS, N_CTX * TOK_DEV, D)

    def forward_all(weights_in, inputs_in):
        return lax.map(lambda single: sequence_forward(single, positions, weights_in), inputs_in)
    outputs, backward = jax.vjp(forward_all, params, sequences)
    grads, grad_inputs = backward(cotangents)
    out_block = jnp.swapaxes(outputs.reshape(SEQS, N_CTX, TOK_DEV, D), 0, 1).astype(jnp.bfloat16)
    grad_tokens = jnp.swapaxes(grad_inputs.reshape(SEQS, N_CTX, TOK_DEV, D), 0, 1).astype(jnp.bfloat16)
    grads = tuple((item.astype(jnp.float32) for item in grads))
    return (out_block, grad_tokens, grads[0], grads[1], grads[2], grads[3], grads[4], grads[5], grads[6], grads[7], grads[8], grads[9], grads[10], grads[11])
```

```python
import jax
import jax.numpy as jnp
from jax import lax
from jax.experimental import pallas as pl
from jax.experimental.pallas import tpu as pltpu
from jax.sharding import PartitionSpec as P

HEADS = 16
HEAD_DIM = 64
ROT_DIMS = 16
EPSILON = 1e-05
NEGATIVE = -1e30
F32 = jnp.float32
BF16 = jnp.bfloat16

Q_TILE = 256
K_TILE = 512


def dot(a, b, ca=1, cb=0):
    return lax.dot_general(a, b, (((ca,), (cb,)), ((), ())), preferred_element_type=F32)


def attention_kernel(order_ref, recv_ref, out_ref, kv, kvt, qz, gz, sbuf, dbuf, dkv):
    blocks = recv_ref.shape[0]
    rows = 128
    half_rows = 64
    tiles = blocks * half_rows // Q_TILE
    per_tile = Q_TILE // half_rows
    half = order_ref[blocks]
    lane = lax.broadcasted_iota(jnp.int32, (half_rows, 128), 1)

    def arrange(b, carry):
        c = order_ref[b]
        kv[pl.ds(pl.multiple_of(b * rows, rows), rows), :] = recv_ref[c, 0:rows, :]
        qg = recv_ref[c, rows : rows + half_rows, :].astype(F32)
        at = pl.ds(pl.multiple_of(b * half_rows, half_rows), half_rows)
        qz[at, :] = jnp.where(lane < HEAD_DIM, qg * (HEAD_DIM**-0.5), 0.0).astype(BF16)
        gz[at, :] = jnp.where(lane < HEAD_DIM, 0.0, qg).astype(BF16)
        return carry

    lax.fori_loop(0, blocks, arrange, 0)

    def turn(j, carry):
        at = pl.ds(pl.multiple_of(j * K_TILE, K_TILE), K_TILE)
        kvt[:, at] = kv[at, :].T
        dkv[at, :] = jnp.zeros((K_TILE, 128), F32)
        return carry

    lax.fori_loop(0, tiles, turn, 0)

    key_row = lax.broadcasted_iota(jnp.int32, (K_TILE, Q_TILE), 0)
    query = lax.broadcasted_iota(jnp.int32, (K_TILE, Q_TILE), 1)
    place = (query // half_rows) * rows + half * half_rows + query % half_rows
    allowed = key_row <= place

    def folded(v, op):
        return op(v.reshape(K_TILE // 8, 8, Q_TILE), axis=0)

    def tile(i, carry):
        q_at = pl.ds(pl.multiple_of(i * Q_TILE, Q_TILE), Q_TILE)
        q = qz[q_at, :]
        g = gz[q_at, :]

        def score(j, top):
            at = pl.ds(pl.multiple_of(j * K_TILE, K_TILE), K_TILE)
            s = dot(kv[at, :], q, 1, 1)
            sbuf[at, :] = s
            return jnp.maximum(top, folded(s, jnp.max))

        top = lax.fori_loop(0, i, score, jnp.full((8, Q_TILE), NEGATIVE, F32))
        last = pl.ds(pl.multiple_of(i * K_TILE, K_TILE), K_TILE)
        s = jnp.where(allowed, dot(kv[last, :], q, 1, 1), NEGATIVE)
        sbuf[last, :] = s
        top = jnp.maximum(top, folded(s, jnp.max))
        top = jnp.max(top, axis=0, keepdims=True)

        def weigh(j, carry):
            total, delta = carry
            at = pl.ds(pl.multiple_of(j * K_TILE, K_TILE), K_TILE)
            p = jnp.exp(sbuf[at, :] - top)
            sbuf[at, :] = p
            dp = dot(kv[at, :], g, 1, 1)
            dbuf[at, :] = dp
            return total + folded(p, jnp.sum), delta + folded(p * dp, jnp.sum)

        zero = jnp.zeros((8, Q_TILE), F32)
        total, delta = lax.fori_loop(0, i + 1, weigh, (zero, zero))
        inverse = 1.0 / jnp.sum(total, axis=0, keepdims=True)
        delta = jnp.sum(delta, axis=0, keepdims=True) * inverse

        def spread(j, carry):
            att, dq = carry
            at = pl.ds(pl.multiple_of(j * K_TILE, K_TILE), K_TILE)
            p = sbuf[at, :] * inverse
            pb = p.astype(BF16)
            ds = (p * (dbuf[at, :] - delta)).astype(BF16)
            kt = kvt[:, at]
            dkv[at, :] = dkv[at, :] + (dot(ds, q) + dot(pb, g))
            return att + dot(kt, pb), dq + dot(kt, ds)

        zeros = jnp.zeros((128, Q_TILE), F32)
        att, dq = lax.fori_loop(0, i + 1, spread, (zeros, zeros))
        feature = lax.broadcasted_iota(jnp.int32, (128, Q_TILE), 0)
        both = jnp.where(feature < HEAD_DIM, dq * (HEAD_DIM**-0.5), att).T.astype(BF16)
        for b in range(per_tile):
            c = order_ref[i * per_tile + b]
            out_ref[c, rows : rows + half_rows, :] = both[b * half_rows : (b + 1) * half_rows, :]
        return carry

    lax.fori_loop(0, tiles, tile, 0)

    def put(b, carry):
        c = order_ref[b]
        at = pl.ds(pl.multiple_of(b * rows, rows), rows)
        out_ref[c, 0:rows, :] = dkv[at, :].astype(BF16)
        return carry

    lax.fori_loop(0, blocks, put, 0)


def attention(order, received):
    blocks = received.shape[0]
    keys = blocks * 128
    queries = blocks * 64
    return pl.pallas_call(
        attention_kernel,
        grid_spec=pltpu.PrefetchScalarGridSpec(
            num_scalar_prefetch=1,
            grid=(),
            in_specs=[pl.BlockSpec(memory_space=pltpu.VMEM)],
            out_specs=pl.BlockSpec(memory_space=pltpu.VMEM),
            scratch_shapes=[
                pltpu.VMEM((keys, 128), BF16),
                pltpu.VMEM((128, keys), BF16),
                pltpu.VMEM((queries, 128), BF16),
                pltpu.VMEM((queries, 128), BF16),
                pltpu.VMEM((keys, Q_TILE), F32),
                pltpu.VMEM((keys, Q_TILE), F32),
                pltpu.VMEM((keys, 128), F32),
            ],
        ),
        out_shape=jax.ShapeDtypeStruct(received.shape, BF16),
        compiler_params=pltpu.CompilerParams(vmem_limit_bytes=40 * 1024 * 1024),
        cost_estimate=pl.CostEstimate(
            flops=keys * queries * 64 * 6, bytes_accessed=2 * received.size * 2, transcendentals=keys * queries // 2
        ),
    )(order, received)


def swap(value, flip):
    return lax.ppermute(value, "fsdp", [(i, i ^ flip) for i in range(4)])


def shuffle(chunk_of, mine):
    own = chunk_of(mine)
    whole = jnp.zeros((4,) + own.shape, own.dtype)
    for flip in range(4):
        other = mine ^ flip
        piece = own if flip == 0 else swap(chunk_of(other), flip)
        whole = lax.dynamic_update_slice(whole, piece[None], (other, 0, 0))
    return whole.reshape(4 * own.shape[0], own.shape[1])


def on_device(
    tokens,
    block_order,
    weight_qkv,
    bias_qkv,
    weight_dense,
    bias_dense,
    weight_up,
    bias_up,
    weight_down,
    bias_down,
    gain_one,
    shift_one,
    gain_two,
    shift_two,
    cotangent,
):
    rows = tokens.shape[2]
    width = tokens.shape[3]
    blocks = lax.axis_size("ctx")
    ctx = lax.axis_index("ctx")
    mine = lax.axis_index("fsdp")
    part = width // 4
    own_tokens = tokens.reshape(rows, width)
    own_cot = cotangent.reshape(rows, width)

    def gather(value):
        across = swap(value, 2)
        return [value, swap(value, 1), across, swap(across, 1)]

    vectors = jnp.concatenate(
        [gain_one, shift_one, gain_two, shift_two, bias_dense, bias_down, bias_qkv, jnp.zeros((768,), BF16)]
    ).reshape(3, width)
    packed = gather(jnp.concatenate([own_tokens, vectors, jnp.zeros((13, width), BF16)], axis=0))
    four_tokens = jnp.concatenate([piece[:rows] for piece in packed], axis=0)
    natural = jnp.arange(4) ^ mine
    vectors = jnp.stack([piece[rows : rows + 3] for piece in packed])[natural].reshape(4, 3 * width)

    def whole_vector(at, size=part):
        return vectors[:, at : at + size].reshape(4 * size).astype(F32)

    gone, sone, gtwo, stwo, bdense, bdown = [whole_vector(part * i) for i in range(6)]
    bqkv = lax.dynamic_slice_in_dim(whole_vector(6 * part, 768).reshape(3, 4, part), mine, 1, axis=1).reshape(768)

    def qkv_chunk(j):
        return jnp.concatenate(
            [lax.dynamic_slice_in_dim(weight_qkv, width * i + part * j, part, axis=1) for i in range(3)], axis=1
        )

    my_qkv = shuffle(qkv_chunk, mine)
    four_cot = jnp.concatenate(gather(own_cot), axis=0)
    my_up = shuffle(lambda j: lax.dynamic_slice_in_dim(weight_up, width * j, width, axis=1), mine)
    my_down = shuffle(lambda j: lax.dynamic_slice_in_dim(weight_down, width * j, width, axis=1), mine)

    inputs = four_tokens.astype(F32)
    centre = inputs - jnp.mean(inputs, axis=-1, keepdims=True)
    spread = lax.rsqrt(jnp.mean(centre * centre, axis=-1, keepdims=True) + EPSILON)
    normal = centre * spread
    low_one = (normal * gone + sone).astype(BF16)
    low_two = (normal * gtwo + stwo).astype(BF16)

    places = (block_order[ctx] * rows + jnp.arange(rows, dtype=jnp.int32)).astype(F32)
    halfway = ROT_DIMS // 2
    inverse = 10000.0 ** (-2.0 * jnp.arange(halfway).astype(F32) / ROT_DIMS)
    phases = places[:, None] * inverse[None, :]
    cos8, sin8 = jnp.cos(phases), jnp.sin(phases)
    zero8 = jnp.zeros_like(sin8)
    rest = jnp.zeros((rows, HEAD_DIM - ROT_DIMS), F32)
    cos_all = jnp.tile(jnp.concatenate([cos8, cos8, rest + 1.0], axis=1), (4, 4))
    sin_low = jnp.tile(jnp.concatenate([-sin8, zero8, rest], axis=1), (4, 4))
    sin_high = jnp.tile(jnp.concatenate([zero8, sin8, rest], axis=1), (4, 4))

    def turn(u, sign):
        return u * cos_all + sign * (
            jnp.roll(u, -halfway, axis=1) * sin_low + jnp.roll(u, halfway, axis=1) * sin_high
        )

    projected = dot(low_one, my_qkv) + bqkv
    queries = turn(projected[:, :part], 1.0).astype(BF16)
    key_rows = turn(projected[:, part : 2 * part], 1.0).astype(BF16)
    values = projected[:, 2 * part :].astype(BF16)
    grad_att = dot(four_cot, weight_dense, 1, 1).astype(BF16)

    def by_head(value):
        return value.reshape(4, rows, 4, HEAD_DIM).transpose(0, 2, 1, 3)

    kv = jnp.concatenate([by_head(key_rows), by_head(values)], axis=-1)
    qg = jnp.concatenate([by_head(queries), by_head(grad_att)], axis=-1).reshape(4, 4, 2, rows // 2, 128)
    message = jnp.concatenate([jnp.broadcast_to(kv[:, :, None], (4, 4, 2, rows, 128)), qg], axis=3)
    received = lax.all_to_all(message.reshape(blocks, 192, 128), "ctx", 0, 0, tiled=True)
    order = jnp.zeros((blocks,), jnp.int32).at[block_order].set(jnp.arange(blocks, dtype=jnp.int32))
    order = jnp.concatenate([order, (ctx % 2).astype(jnp.int32)[None]])
    answer = attention(order, received)
    back = lax.all_to_all(answer, "ctx", 0, 0, tiled=True).reshape(4, 4, 2, 192, 128)

    upward = dot(low_two, my_up) + bias_up.astype(F32)
    activated, gelu_back = jax.vjp(lambda v: jax.nn.gelu(v, approximate=False), upward)
    act_low = activated.astype(BF16)
    grad_act = dot(four_cot, my_down)
    grad_up = gelu_back(grad_act)[0].astype(BF16)
    mlp_out = dot(act_low, my_down, 1, 1)
    grad_two = dot(grad_up, my_up, 1, 1)
    gup = dot(low_two, grad_up, 0, 0)
    gdown = dot(four_cot, act_low, 0, 0)

    dkv = jnp.sum(back[:, :, :, :rows].astype(F32), axis=2)
    qa = back[:, :, :, rows:].reshape(4, 4, rows, 128)

    def by_token(value):
        return value.transpose(0, 2, 1, 3).reshape(4 * rows, part)

    att = by_token(qa[..., HEAD_DIM:])
    grad_qkv = jnp.concatenate(
        [
            turn(by_token(qa[..., :HEAD_DIM]).astype(F32), -1.0),
            turn(by_token(dkv[..., :HEAD_DIM]), -1.0),
            by_token(dkv[..., HEAD_DIM:]),
        ],
        axis=1,
    ).astype(BF16)
    grad_one = dot(grad_qkv, my_qkv, 1, 1)
    gqkv = dot(low_one, grad_qkv, 0, 0)
    gdense = dot(att, four_cot, 0, 0)

    def norm_back(grad, gain):
        e = grad * gain
        return spread * (
            e - jnp.mean(e, axis=-1, keepdims=True) - normal * jnp.mean(e * normal, axis=-1, keepdims=True)
        )

    out_part = mlp_out + dot(att, weight_dense)
    in_part = norm_back(grad_one, gone) + norm_back(grad_two, gtwo)

    def collect(partial):
        low = partial.astype(BF16)
        total = partial[:rows]
        for flip in range(1, 4):
            total = total + swap(low[flip * rows : (flip + 1) * rows], flip).astype(F32)
        return total

    both = collect(jnp.concatenate([out_part, in_part], axis=1))
    out_block = (own_tokens.astype(F32) + both[:, :width] + (bdense + bdown)).astype(BF16)
    grad_tokens = (own_cot.astype(F32) + both[:, width:]).astype(BF16)

    def owners(value):
        return value.reshape(4, blocks, 8, value.shape[1]).transpose(1, 0, 2, 3).astype(BF16)

    cot32 = four_cot.astype(F32)
    sum_cot = lax.dynamic_slice_in_dim(jnp.sum(cot32, axis=0), mine * part, part)
    norms = jnp.stack(
        [
            jnp.sum(grad_one * normal, axis=0),
            jnp.sum(grad_one, axis=0),
            jnp.sum(grad_two * normal, axis=0),
            jnp.sum(grad_two, axis=0),
        ]
    )
    norms = norms.reshape(4, 4, blocks, 8).transpose(2, 1, 0, 3).reshape(blocks, 4, 32)
    sum_qkv = jnp.sum(grad_qkv.astype(F32), axis=0).reshape(blocks, 1, 24)
    sum_up = jnp.sum(grad_up.astype(F32), axis=0).reshape(blocks, 4, 8)
    small = jnp.concatenate(
        [
            norms,
            jnp.broadcast_to(sum_qkv, (blocks, 4, 24)),
            sum_up,
            sum_cot.reshape(blocks, 4, 2),
            jnp.zeros((blocks, 4, 62), F32),
        ],
        axis=2,
    )
    small = jnp.pad(small[:, :, None, :], ((0, 0), (0, 0), (0, 7), (0, 0))).astype(BF16)
    dense_piece = gdense.reshape(blocks, 8, 4, part).transpose(0, 2, 1, 3).astype(BF16)
    outgoing = jnp.concatenate([owners(gqkv), owners(gup), owners(gdown), dense_piece, small], axis=3)
    arrived = lax.all_to_all(outgoing, "ctx", 0, 0, tiled=True)
    summed = jnp.sum(arrived.astype(F32), axis=0).astype(BF16)
    crossed = lax.all_to_all(summed, "fsdp", 0, 0, tiled=True)
    up_at, down_at, dense_at, small_at = 768, 768 + width, 768 + 2 * width, 1024 + 2 * width
    mat_qkv = crossed[:, :, :768].reshape(4, 8, 3, part).transpose(1, 2, 0, 3).reshape(8, 3 * width)
    mat_up = crossed[:, :, up_at:down_at].transpose(1, 0, 2).reshape(8, 4 * width)
    mat_down = crossed[:, :, down_at:dense_at].transpose(1, 0, 2).reshape(8, 4 * width)
    mat_dense = summed[:, :, dense_at:small_at].transpose(1, 0, 2).reshape(8, width)
    vec_norm = jnp.sum(crossed[:, 0, small_at : small_at + 32].astype(F32), axis=0).astype(BF16)
    vec_qkv = crossed[:, 0, small_at + 32 : small_at + 56].reshape(96)
    vec_up = summed[:, 0, small_at + 56 : small_at + 64].reshape(32)
    vec_cot = summed[:, 0, small_at + 64 : small_at + 66].reshape(8)
    vec = jnp.concatenate([vec_norm, vec_qkv, vec_up, vec_cot, jnp.zeros((88,), BF16)])
    vec = jnp.pad(vec[None], ((0, 7), (0, 0)))
    chunk = jnp.concatenate([mat_qkv, mat_dense, mat_up, mat_down, vec], axis=1)
    full = lax.all_to_all(jnp.broadcast_to(chunk[None], (blocks,) + chunk.shape), "ctx", 0, 0, tiled=True)
    full = full.reshape(blocks * 8, chunk.shape[1])

    def columns(at, size):
        return full[:, at : at + size].astype(F32)

    g_qkv = columns(0, 3 * width)
    g_dense = columns(3 * width, width)
    g_up = columns(4 * width, 4 * width)
    g_down = columns(8 * width, 4 * width)
    vec = full.reshape(blocks, 8, chunk.shape[1])[:, 0, 12 * width :].astype(F32)
    g_norm = vec[:, :32].reshape(blocks, 4, 8).transpose(1, 0, 2).reshape(4, part)
    g_bqkv = vec[:, 32:128].reshape(blocks, 4, 24).transpose(1, 0, 2).reshape(4, 3, part)
    g_bqkv = lax.dynamic_slice_in_dim(g_bqkv.transpose(1, 0, 2).reshape(3 * width), mine * 768, 768)
    g_bup = vec[:, 128:160].reshape(width)
    g_cot = vec[:, 160:168].reshape(part)
    return (
        out_block.reshape(tokens.shape),
        grad_tokens.reshape(tokens.shape),
        g_qkv,
        g_bqkv,
        g_dense,
        g_cot,
        g_up,
        g_bup,
        g_down,
        g_cot,
        g_norm[0],
        g_norm[1],
        g_norm[2],
        g_norm[3],
    )


def solution(mesh):
    block = P("ctx", "fsdp", None, None)
    matrix = P("fsdp", None)
    vector = P("fsdp")
    return jax.shard_map(
        on_device,
        mesh=mesh,
        in_specs=(
            block,
            P(),
            matrix,
            vector,
            matrix,
            vector,
            matrix,
            vector,
            matrix,
            vector,
            vector,
            vector,
            vector,
            vector,
            block,
        ),
        out_specs=(
            block,
            block,
            matrix,
            vector,
            matrix,
            vector,
            matrix,
            vector,
            matrix,
            vector,
            vector,
            vector,
            vector,
            vector,
        ),
        check_vma=False,
    )
```

```python
import jax
import jax.numpy as jnp
from jax import lax
from jax.experimental import pallas as pl
from jax.experimental.pallas import tpu as pltpu
from jax.sharding import PartitionSpec as P

HEADS = 16
HEAD_DIM = 64
ROT_DIMS = 16
EPSILON = 1e-05
NEGATIVE = -1e30
F32 = jnp.float32
BF16 = jnp.bfloat16

Q_TILE = 256
K_TILE = 512


def dot(a, b, ca=1, cb=0):
    return lax.dot_general(a, b, (((ca,), (cb,)), ((), ())), preferred_element_type=F32)


def attention_kernel(order_ref, recv_ref, out_ref, kv, kvt, qz, gz, sbuf, dbuf, dkv):
    blocks = recv_ref.shape[0]
    rows = 128
    half_rows = 64
    tiles = blocks * half_rows // Q_TILE
    per_tile = Q_TILE // half_rows
    half = order_ref[blocks]
    lane = lax.broadcasted_iota(jnp.int32, (half_rows, 128), 1)

    def arrange(b, carry):
        c = order_ref[b]
        kv[pl.ds(pl.multiple_of(b * rows, rows), rows), :] = recv_ref[c, 0:rows, :]
        qg = recv_ref[c, rows : rows + half_rows, :].astype(F32)
        at = pl.ds(pl.multiple_of(b * half_rows, half_rows), half_rows)
        qz[at, :] = jnp.where(lane < HEAD_DIM, qg * (HEAD_DIM**-0.5), 0.0).astype(BF16)
        gz[at, :] = jnp.where(lane < HEAD_DIM, 0.0, qg).astype(BF16)
        return carry

    lax.fori_loop(0, blocks, arrange, 0)

    def turn(j, carry):
        at = pl.ds(pl.multiple_of(j * K_TILE, K_TILE), K_TILE)
        kvt[:, at] = kv[at, :].T
        dkv[at, :] = jnp.zeros((K_TILE, 128), F32)
        return carry

    lax.fori_loop(0, tiles, turn, 0)

    key_row = lax.broadcasted_iota(jnp.int32, (K_TILE, Q_TILE), 0)
    query = lax.broadcasted_iota(jnp.int32, (K_TILE, Q_TILE), 1)
    place = (query // half_rows) * rows + half * half_rows + query % half_rows
    allowed = key_row <= place

    def folded(v, op):
        return op(v.reshape(K_TILE // 8, 8, Q_TILE), axis=0)

    def tile(i, carry):
        q_at = pl.ds(pl.multiple_of(i * Q_TILE, Q_TILE), Q_TILE)
        q = qz[q_at, :]
        g = gz[q_at, :]

        def score(j, top):
            at = pl.ds(pl.multiple_of(j * K_TILE, K_TILE), K_TILE)
            s = dot(kv[at, :], q, 1, 1)
            sbuf[at, :] = s
            return jnp.maximum(top, folded(s, jnp.max))

        top = lax.fori_loop(0, i, score, jnp.full((8, Q_TILE), NEGATIVE, F32))
        last = pl.ds(pl.multiple_of(i * K_TILE, K_TILE), K_TILE)
        s = jnp.where(allowed, dot(kv[last, :], q, 1, 1), NEGATIVE)
        sbuf[last, :] = s
        top = jnp.maximum(top, folded(s, jnp.max))
        top = jnp.max(top, axis=0, keepdims=True)

        def weigh(j, carry):
            total, delta = carry
            at = pl.ds(pl.multiple_of(j * K_TILE, K_TILE), K_TILE)
            p = jnp.exp(sbuf[at, :] - top)
            sbuf[at, :] = p
            dp = dot(kv[at, :], g, 1, 1)
            dbuf[at, :] = dp
            return total + folded(p, jnp.sum), delta + folded(p * dp, jnp.sum)

        zero = jnp.zeros((8, Q_TILE), F32)
        total, delta = lax.fori_loop(0, i + 1, weigh, (zero, zero))
        inverse = 1.0 / jnp.sum(total, axis=0, keepdims=True)
        delta = jnp.sum(delta, axis=0, keepdims=True) * inverse

        def spread(j, carry):
            att, dq = carry
            at = pl.ds(pl.multiple_of(j * K_TILE, K_TILE), K_TILE)
            p = sbuf[at, :] * inverse
            pb = p.astype(BF16)
            ds = (p * (dbuf[at, :] - delta)).astype(BF16)
            kt = kvt[:, at]
            dkv[at, :] = dkv[at, :] + (dot(ds, q) + dot(pb, g))
            return att + dot(kt, pb), dq + dot(kt, ds)

        zeros = jnp.zeros((128, Q_TILE), F32)
        att, dq = lax.fori_loop(0, i + 1, spread, (zeros, zeros))
        feature = lax.broadcasted_iota(jnp.int32, (128, Q_TILE), 0)
        both = jnp.where(feature < HEAD_DIM, dq * (HEAD_DIM**-0.5), att).T.astype(BF16)
        for b in range(per_tile):
            c = order_ref[i * per_tile + b]
            out_ref[c, rows : rows + half_rows, :] = both[b * half_rows : (b + 1) * half_rows, :]
        return carry

    lax.fori_loop(0, tiles, tile, 0)

    def put(b, carry):
        c = order_ref[b]
        at = pl.ds(pl.multiple_of(b * rows, rows), rows)
        out_ref[c, 0:rows, :] = dkv[at, :].astype(BF16)
        return carry

    lax.fori_loop(0, blocks, put, 0)


def attention(order, received):
    blocks = received.shape[0]
    keys = blocks * 128
    queries = blocks * 64
    return pl.pallas_call(
        attention_kernel,
        grid_spec=pltpu.PrefetchScalarGridSpec(
            num_scalar_prefetch=1,
            grid=(),
            in_specs=[pl.BlockSpec(memory_space=pltpu.VMEM)],
            out_specs=pl.BlockSpec(memory_space=pltpu.VMEM),
            scratch_shapes=[
                pltpu.VMEM((keys, 128), BF16),
                pltpu.VMEM((128, keys), BF16),
                pltpu.VMEM((queries, 128), BF16),
                pltpu.VMEM((queries, 128), BF16),
                pltpu.VMEM((keys, Q_TILE), F32),
                pltpu.VMEM((keys, Q_TILE), F32),
                pltpu.VMEM((keys, 128), F32),
            ],
        ),
        out_shape=jax.ShapeDtypeStruct(received.shape, BF16),
        compiler_params=pltpu.CompilerParams(vmem_limit_bytes=40 * 1024 * 1024),
        cost_estimate=pl.CostEstimate(
            flops=keys * queries * 64 * 6, bytes_accessed=2 * received.size * 2, transcendentals=keys * queries // 2
        ),
    )(order, received)


def prepare_kernel(
    ids, x0, x1, x2, x3, w0, w1, w2, w3, w4, w5, dense, cosine, sine_low, sine_high,
    send, low_one, low_two, cots, w_all, vec, bias, proj, att,
):
    rows, part = 128, 256
    natural_weight(ids, (w0, w1, w2, w3, w4, w5), w_all)
    for k, x in enumerate((x0, x1, x2, x3)):
        small = x[rows : rows + 16, :].astype(F32)
        for i in range(6):
            place = slice(part * (i % 4), part * (i % 4 + 1))
            vec[i : i + 1, pl.ds(pl.multiple_of(part * ids[k], part), part)] = small[i // 4 : i // 4 + 1, place]
        for i, place in enumerate(((1, 2), (1, 3), (2, 0))):
            piece = small[place[0] : place[0] + 1, part * place[1] : part * (place[1] + 1)]
            bias[:, pl.ds(pl.multiple_of(768 * ids[k] + part * i, part), part)] = piece
    gone, sone, gtwo, stwo = (vec[i : i + 1, :] for i in range(4))
    for k, x in enumerate((x0, x1, x2, x3)):
        normal, _ = normalise(x[0:rows, :])
        at = slice(k * rows, (k + 1) * rows)
        low_one[at, :] = (normal * gone + sone).astype(BF16)
        low_two[at, :] = (normal * gtwo + stwo).astype(BF16)
    for k, x in enumerate((x0, x1, x2, x3)):
        cots[k * rows : (k + 1) * rows, :] = x[rows + 16 :, :]
    proj[...] = dot(low_one[...], w_all[...])
    att[...] = dot(cots[...], dense[...], 1, 1)
    mine = ids[0]
    biases = [bias[0:1, pl.ds(pl.multiple_of(1024 * i + part * mine, part), part)] for i in range(3)]
    lane = lax.broadcasted_iota(jnp.int32, (rows, 128), 1)
    first = lane < HEAD_DIM
    for k in range(4):
        at = slice(k * rows, (k + 1) * rows)
        qkv = [proj[at, part * i : part * (i + 1)] + biases[i] for i in range(3)]
        query = turned(qkv[0], cosine[...], sine_low[...], sine_high[...])
        key = turned(qkv[1], cosine[...], sine_low[...], sine_high[...])
        grads = att[at, :]
        for p in range(2):
            lanes = slice(128 * p, 128 * (p + 1))
            q, kk, v, a = query[:, lanes], key[:, lanes], qkv[2][:, lanes], grads[:, lanes]
            pairs = (
                (jnp.where(first, kk, pltpu.roll(v, 64, 1)), jnp.where(first, q, pltpu.roll(a, 64, 1))),
                (jnp.where(first, pltpu.roll(kk, 64, 1), v), jnp.where(first, pltpu.roll(q, 64, 1), a)),
            )
            for odd, (kv, qg) in enumerate(pairs):
                base = (4 * k + 2 * p + odd) * 2
                kv, qg = kv.astype(BF16), qg.astype(BF16)
                send[base, 0:128, :] = kv
                send[base + 1, 0:128, :] = kv
                send[base, 128:192, :] = qg[0:64, :]
                send[base + 1, 128:192, :] = qg[64:128, :]


def natural_weight(ids, pieces, whole):
    own, core, far_two, far_three, by_y, by_z = pieces
    for k, piece in ((0, own), (1, core)):
        whole[pl.ds(pl.multiple_of(256 * ids[k], 256), 256), :] = piece[...]
    for k, piece in ((2, far_two), (3, far_three)):
        start = 256 * ids[k]
        whole[pl.ds(pl.multiple_of(start + 128 * ids[4], 128), 128), :] = piece[...]
        other = start + 128 * (1 - ids[4])
        quarter = slice(64 * (k - 2), 64 * (k - 1))
        whole[pl.ds(pl.multiple_of(other, 64), 64), :] = by_y[quarter, :]
        whole[pl.ds(pl.multiple_of(other + 64, 64), 64), :] = by_z[quarter, :]


def normalise(value):
    value = value.astype(F32)
    centre = value - jnp.mean(value, axis=-1, keepdims=True)
    spread = lax.rsqrt(jnp.mean(centre * centre, axis=-1, keepdims=True) + EPSILON)
    return centre * spread, spread


def turned(u, cosine, sine_low, sine_high):
    halfway = ROT_DIMS // 2
    size = u.shape[1]
    return u * cosine + pltpu.roll(u, size - halfway, 1) * sine_low + pltpu.roll(u, halfway, 1) * sine_high


def feed_kernel(
    ids, low_one, low_two, cots, u0, u1, u2, u3, u4, u5, d0, d1, d2, d3, d4, d5, bias_up,
    by_z, y0, y1, y2, y3, mlp_out, grad_two, sum_up, one_t, up, down, two_t, cots_t,
):
    part = 256
    natural_weight(ids, (u0, u1, u2, u3, u4, u5), up)
    natural_weight(ids, (d0, d1, d2, d3, d4, d5), down)
    for i in range(4):
        at = slice(part * i, part * (i + 1))
        two_t[at, :] = low_two[:, at].T
        turned_cots = cots[:, at].T
        for x in range(2):
            for y in range(4):
                to = part * ids[i] + 64 * ids[5 + y] + 32 * x
                cots_t[pl.ds(pl.multiple_of(to, 32), 32), :] = turned_cots[128 * x + 32 * y : 128 * x + 32 * y + 32, :]
        one_t[at, :] = low_one[:, at].T
    for i in range(4):
        at = slice(part * i, part * (i + 1))
        pre = dot(low_two[...], up[:, at]) + bias_up[0:1, at]
        cdf = 0.5 * (1.0 + lax.erf(pre * (0.5**0.5)))
        slope = cdf + pre * (jnp.exp(-0.5 * pre * pre) * 0.3989422804014327)
        act = (pre * cdf).astype(BF16)
        grad = (dot(cots[...], down[:, at]) * slope).astype(BF16)
        out = dot(act, down[:, at], 1, 1)
        back = dot(grad, up[:, at], 1, 1)
        if i == 0:
            mlp_out[...] = out
            grad_two[...] = back
        else:
            mlp_out[...] = mlp_out[...] + out
            grad_two[...] = grad_two[...] + back
        sum_up[:, at] = jnp.sum(grad.astype(F32).reshape(64, 8, part), axis=0)
        for pair in range(2):
            gup, gdown = [], []
            for k in (2 * pair, 2 * pair + 1):
                owner = pl.ds(pl.multiple_of(part * ids[k], part), part)
                gup.append(dot(two_t[owner, :], grad).reshape(2, 4, 4, 8, part))
                gdown.append(dot(cots_t[part * k : part * (k + 1), :], act).reshape(4, 8, 8, part))
            for n in range(4):
                piece = jnp.concatenate([v[:, :, n] for v in gup], axis=2).reshape(8, 16, part)
                by_z[n, :, pair, :, at] = piece.astype(BF16)
                piece = jnp.concatenate([v[n] for v in gdown], axis=1)
                (y0, y1, y2, y3)[n][:, pair, :, at] = piece.astype(BF16)


def finish_kernel(
    ids, back, w_all, dense, x0, x1, x2, x3, vec, cosine, sine_low, sine_high, one_t, cots, mlp_out, grad_two, sum_up,
    message, own_part, sent, grads, att, g_one, sums, dense_grad,
):
    rows, part = 128, 256
    lane = lax.broadcasted_iota(jnp.int32, (rows, 128), 1)
    first = lane < HEAD_DIM
    for k in range(4):
        at = slice(k * rows, (k + 1) * rows)
        pieces = [[], [], [], []]
        for p in range(2):
            kvs, qas = [], []
            for odd in range(2):
                base = (4 * k + 2 * p + odd) * 2
                kvs.append(back[base, 0:128, :].astype(F32) + back[base + 1, 0:128, :].astype(F32))
                qas.append(
                    jnp.concatenate([back[base, 128:192, :].astype(F32), back[base + 1, 128:192, :].astype(F32)], axis=0)
                )
            for into, pair in ((pieces[1], kvs), (pieces[0], qas)):
                into.append(jnp.where(first, pair[0], pltpu.roll(pair[1], 64, 1)))
            for into, pair in ((pieces[2], kvs), (pieces[3], qas)):
                into.append(jnp.where(first, pltpu.roll(pair[0], 64, 1), pair[1]))
        dq, dk, dv, out = (jnp.concatenate(piece, axis=1) for piece in pieces)
        dq = turned(dq, cosine[...], -sine_low[...], -sine_high[...])
        dk = turned(dk, cosine[...], -sine_low[...], -sine_high[...])
        grads[at, 0:part] = dq.astype(BF16)
        grads[at, part : 2 * part] = dk.astype(BF16)
        grads[at, 2 * part :] = dv.astype(BF16)
        att[at, :] = out.astype(BF16)
    dense_grad[...] = dot(att[...], cots[...], 0, 0).reshape(32, 8, 4 * part)
    for k in range(4):
        owner = pl.ds(pl.multiple_of(part * ids[k], part), part)
        gqkv = dot(one_t[owner, :], grads[...]).reshape(32, 8, 3 * part)
        lower = jnp.concatenate([gqkv[:, :, 512:], dense_grad[:, :, owner]], axis=2)
        message[:, :, pl.ds(pl.multiple_of(512 * ids[k], 512), 512)] = jnp.concatenate([gqkv[:, :, :512], lower], axis=1).astype(BF16)
    g_one[...] = dot(grads[...], w_all[...], 1, 1)
    gone, gtwo = vec[0:1, :], vec[2:3, :]
    biases = vec[4:5, :] + vec[5:6, :]
    folded = [jnp.zeros((8, 4 * part), F32) for _ in range(5)]
    for k, x in enumerate((x0, x1, x2, x3)):
        at = slice(k * rows, (k + 1) * rows)
        normal, spread = normalise(x[0:rows, :])
        one, two = g_one[at, :], grad_two[at, :]
        cot = cots[at, :].astype(F32)
        for i, value in enumerate((one * normal, one, two * normal, two, cot)):
            folded[i] = folded[i] + jnp.sum(value.reshape(16, 8, 4 * part), axis=0)
        e = one * gone + two * gtwo
        inner = spread * (
            e - jnp.mean(e, axis=-1, keepdims=True) - normal * jnp.mean(e * normal, axis=-1, keepdims=True)
        )
        outer = mlp_out[at, :] + dot(att[at, :], dense[...])
        if k == 0:
            own_part[:, 0 : 4 * part] = outer + x[0:rows, :].astype(F32) + biases
            own_part[:, 4 * part :] = inner + cot
        else:
            slot = (None, 0, 2, 1)[k]
            sent[slot, :, 0 : 4 * part] = outer.astype(BF16)
            sent[slot, :, 4 * part :] = inner.astype(BF16)
    row = lax.broadcasted_iota(jnp.int32, (16, 128), 0)

    def put(v, values):
        block = jnp.zeros((16, 128), F32)
        for k, value in enumerate(values):
            block = jnp.where(row == 4 * ids[k], value[:, 0:128], block)
            block = jnp.where(row == 4 * ids[k] + 1, value[:, 128:256], block)
        message[v, :, 2048:2176] = block.astype(BF16)

    sums[...] = jnp.zeros_like(sums)
    for i in range(5):
        sums[i : i + 1, :] = jnp.sum(folded[i], axis=0, keepdims=True)
    message[:, :, 2048:2176] = jnp.zeros((32, 16, 128), BF16)
    total = jnp.sum(grads[...].astype(F32), axis=0, keepdims=True)
    ups = jnp.sum(sum_up[...], axis=0, keepdims=True)
    owners = [pl.ds(pl.multiple_of(part * ids[k], part), part) for k in range(4)]
    for v in range(4):
        put(v, [sums[v : v + 1, owner] for owner in owners])
    for v in range(3):
        put(4 + v, [total[:, part * v : part * (v + 1)]] * 4)
    put(7, [sums[4:5, owner] for owner in owners])
    for v in range(4):
        put(8 + v, [ups[:, part * v : part * (v + 1)]] * 4)


def place_kernel(ids, u0, u1, u2, v2, u3, d0, d1, d2, e2, d3, up, down):
    width = 2048

    def put(piece, out, flip, y, z):
        y, z = lax.rem(ids[0] + 4 - y, 4), lax.rem(ids[1] + 4 - z, 4)
        at = pl.ds(pl.multiple_of(8 * (16 * flip + 4 * y + z), 8), 8)
        value = piece.astype(F32)
        out[at, 0:width] = value[0:8, :]
        out[at, width:] = value[8:16, :]

    for d, (one, two) in enumerate(((u0, d0), (u1, d1), ((u2, v2), (d2, e2)), (u3, d3))):
        for e in range(4):
            for flip in range(2):
                if d == 2:
                    put(one[e // 2][e % 2, flip], up, flip, e, d)
                    put(two[e // 2][e % 2, flip], down, flip, d, e)
                else:
                    put(one[e, flip], up, flip, e, d)
                    put(two[e, flip], down, flip, d, e)


def local(kernel, ids, inputs, outs, scratch, limit, flops):
    shapes = [jax.ShapeDtypeStruct(shape, dtype) for shape, dtype in outs]
    moved = sum(v.size * v.dtype.itemsize for v in list(inputs) + shapes)
    return pl.pallas_call(
        kernel,
        grid_spec=pltpu.PrefetchScalarGridSpec(
            num_scalar_prefetch=1,
            grid=(),
            in_specs=[pl.BlockSpec(memory_space=pltpu.VMEM)] * len(inputs),
            out_specs=[pl.BlockSpec(memory_space=pltpu.VMEM)] * len(outs),
            scratch_shapes=[pltpu.VMEM(shape, dtype) for shape, dtype in scratch],
        ),
        out_shape=shapes,
        compiler_params=pltpu.CompilerParams(vmem_limit_bytes=limit * 1024 * 1024),
        cost_estimate=pl.CostEstimate(flops=flops, bytes_accessed=moved, transcendentals=0),
    )(ids, *inputs)


def swap(value, flip):
    return lax.ppermute(value, "fsdp", [(i, i ^ flip) for i in range(4)])


def across(value, flip_ctx, flip):
    order = [(4 * c + f, 4 * (c ^ flip_ctx) + (f ^ flip)) for c in range(32) for f in range(4)]
    return lax.ppermute(value, ("ctx", "fsdp"), order)


def along(value, axis, steps):
    order = []
    for c in range(32):
        x, y, z = c // 16, (c // 4) % 4, c % 4
        to = (x, (y + steps) % 4, z) if axis == "y" else (x, y, (z + steps) % 4)
        order.append((c, 16 * to[0] + 4 * to[1] + to[2]))
    return lax.ppermute(value, "ctx", order)


def shuffle_far(block, ids):
    return [across(block(ids[k], 128 * (1 - ids[4]), 128), 16, k) for k in (2, 3)]


def shuffle_near(block, ids, far, steps):
    own, core = block(ids[0], 0, 256), swap(block(ids[1], 0, 256), 1)
    by_y = along(jnp.concatenate([piece[:64] for piece in far]), "y", steps)
    by_z = along(jnp.concatenate([piece[64:] for piece in far]), "z", steps)
    return [own, core, *far, by_y, by_z]


def on_device(
    tokens,
    block_order,
    weight_qkv,
    bias_qkv,
    weight_dense,
    bias_dense,
    weight_up,
    bias_up,
    weight_down,
    bias_down,
    gain_one,
    shift_one,
    gain_two,
    shift_two,
    cotangent,
):
    rows = tokens.shape[2]
    width = tokens.shape[3]
    blocks = lax.axis_size("ctx")
    ctx = lax.axis_index("ctx").astype(jnp.int32)
    mine = lax.axis_index("fsdp").astype(jnp.int32)
    part = width // 4
    at_x, at_y, at_z = ctx // 16, (ctx // 4) % 4, ctx % 4
    ids = jnp.stack([mine, mine ^ 1, mine ^ 2, mine ^ 3, (at_x + at_y + at_z) % 2] + [(n - at_y) % 4 for n in range(4)])
    own_tokens = tokens.reshape(rows, width)
    own_cot = cotangent.reshape(rows, width)

    def gather(value):
        over = swap(value, 2)
        return [value, swap(value, 1), over, swap(over, 1)]

    def qkv_block(j, start, count):
        return jnp.concatenate(
            [lax.dynamic_slice(weight_qkv, (start, width * i + part * j), (count, part)) for i in range(3)], axis=1
        )

    vectors = jnp.concatenate(
        [gain_one, shift_one, gain_two, shift_two, bias_dense, bias_down, bias_qkv, jnp.zeros((13 * width + 768,), BF16)]
    ).reshape(16, width)
    qkv_far = shuffle_far(qkv_block, ids)
    packed = gather(jnp.concatenate([own_tokens, vectors, own_cot], axis=0))
    first_up, far_over = lax.optimization_barrier((weight_up, packed[2]))
    packed[2] = far_over

    def block_of(weight):
        return lambda j, start, count: lax.dynamic_slice(weight, (start, width * j), (count, width))

    up_far = shuffle_far(block_of(first_up), ids)
    qkv_pieces = shuffle_near(qkv_block, ids, qkv_far, 1)
    first_down, late_up, near_y, near_z = lax.optimization_barrier((weight_down, weight_up, *qkv_pieces[4:]))
    qkv_pieces[4:] = [near_y, near_z]
    down_far = shuffle_far(block_of(first_down), ids)

    places = (block_order[ctx] * rows + lax.broadcasted_iota(jnp.int32, (rows, part), 0)).astype(F32)
    lane = lax.broadcasted_iota(jnp.int32, (rows, part), 1) % HEAD_DIM
    halfway = ROT_DIMS // 2
    inverse = 10000.0 ** (-2.0 * (lane % halfway).astype(F32) / ROT_DIMS)
    phases = jnp.where(lane < ROT_DIMS, places * inverse, 0.0)
    sines = jnp.sin(phases)
    tables = [
        jnp.cos(phases),
        jnp.where(lane < halfway, -sines, 0.0),
        jnp.where(lane < halfway, 0.0, sines),
    ]

    message, low_one, low_two, four_cot, my_qkv, vec = local(
        prepare_kernel,
        ids,
        [*packed, *qkv_pieces, weight_dense, *tables],
        [
            ((blocks, 192, 128), BF16),
            ((4 * rows, width), BF16),
            ((4 * rows, width), BF16),
            ((4 * rows, width), BF16),
            ((width, 3 * part), BF16),
            ((8, width), F32),
        ],
        [((1, 3 * width), F32), ((4 * rows, 3 * part), F32), ((4 * rows, part), F32)],
        60,
        2 * 4 * rows * width * width,
    )
    up_pieces = shuffle_near(block_of(late_up), ids, up_far, 1)
    message, up_pieces, down_far = lax.optimization_barrier((message, up_pieces, down_far))
    feed_pieces = up_pieces + shuffle_near(block_of(first_down), ids, down_far, 3)
    received = lax.all_to_all(message, "ctx", 0, 0, tiled=True)
    order = jnp.zeros((blocks,), jnp.int32).at[block_order].set(jnp.arange(blocks, dtype=jnp.int32))
    order = jnp.concatenate([order, (ctx % 2)[None]])

    by_z, y0, y1, y2, y3, mlp_out, grad_two, sum_up, one_t = local(
        feed_kernel,
        ids,
        [low_one, low_two, four_cot, *feed_pieces, bias_up.astype(F32).reshape(1, width)],
        [
            ((4, 8, 2, 16, width), BF16),
            ((8, 2, 16, width), BF16),
            ((8, 2, 16, width), BF16),
            ((8, 2, 16, width), BF16),
            ((8, 2, 16, width), BF16),
            ((4 * rows, width), F32),
            ((4 * rows, width), F32),
            ((8, width), F32),
            ((width, 4 * rows), BF16),
        ],
        [((width, width), BF16), ((width, width), BF16), ((width, 4 * rows), BF16), ((width, 4 * rows), BF16)],
        60,
        12 * 4 * rows * width * width,
    )
    natural = jnp.arange(4) ^ mine

    def spread(chunk):
        copies = jnp.broadcast_to(chunk[None], (blocks,) + chunk.shape)
        return lax.all_to_all(copies, "ctx", 0, 0, tiled=True).reshape(blocks * chunk.shape[0], chunk.shape[1])

    def added(pieces):
        total = pieces[0].astype(F32)
        for piece in pieces[1:]:
            total = total + piece.astype(F32)
        return total.astype(BF16)

    def pick(value, axis, n):
        return lax.dynamic_index_in_dim(value, n, axis, keepdims=False)

    received, by_z, y0, y1, y2, y3 = lax.optimization_barrier((received, by_z, y0, y1, y2, y3))
    groups = [[4 * n + z for z in range(4)] for n in range(8)]
    up_in = lax.all_to_all(by_z, "ctx", 0, 0, tiled=True, axis_index_groups=groups)
    down_in = [y0] + [along(y, "y", d + 1) for d, y in enumerate((y1, y2, y3))]
    answer = attention(order, received)
    answer, up_in, down_in = lax.optimization_barrier((answer, up_in, down_in))
    up_sum = added([up_in[n] for n in range(4)]).reshape(2, 4, 2, 16, width)
    down_sum = added(down_in).reshape(2, 4, 2, 16, width)
    answer, up_sum, down_sum = lax.optimization_barrier((answer, up_sum, down_sum))

    up_in = [pick(up_sum, 1, at_y)] + [along(pick(up_sum, 1, (at_y + d) % 4), "y", d) for d in range(1, 4)]
    down_in = [pick(down_sum, 1, at_z)] + [along(pick(down_sum, 1, (at_z + d) % 4), "z", d) for d in range(1, 4)]
    back = lax.all_to_all(answer, "ctx", 0, 0, tiled=True)
    feed_sum = jnp.stack([added(up_in), added(down_in)], axis=1)
    back, feed_sum = lax.optimization_barrier((back, feed_sum))

    feed_slots = feed_sum.reshape(2, 2, 4, 8, width)
    feed_cross = [feed_slots[:, :, 0]] + [swap(feed_slots[:, :, k], k) for k in range(1, 4)]
    feed_cross = jnp.stack(feed_cross)[natural]

    tail, own_part, sent = local(
        finish_kernel,
        ids,
        [back, my_qkv, weight_dense, *packed, vec, *tables, one_t, four_cot, mlp_out, grad_two, sum_up],
        [((blocks, 16, 2176), BF16), ((rows, 2 * width), F32), ((3, rows, 2 * width), BF16)],
        [((4 * rows, 3 * part), BF16), ((4 * rows, part), BF16), ((4 * rows, width), F32), ((8, width), F32), ((32, 8, width), F32)],
        60,
        5 * 4 * rows * width * width,
    )
    tail, feed_cross = lax.optimization_barrier((tail, feed_cross))
    feed_pair = added([feed_cross, across(feed_cross, 16, 0)]).reshape(2, 2, 2, 2, 8, width)
    feed_pair = feed_pair.transpose(3, 2, 0, 4, 1, 5).reshape(2, 2, 16, 2 * width)
    tail_arrived = lax.all_to_all(tail, "ctx", 0, 0, tiled=True)

    near = swap(sent[:2], 1).astype(F32)
    both = own_part + near[0] + swap((sent[2].astype(F32) + near[1]).astype(BF16), 2).astype(F32)
    out_block, grad_tokens = both[:, :width].astype(BF16), both[:, width:].astype(BF16)

    up_four = jnp.stack([feed_pair[0]] + [along(feed_pair[0], "y", d) for d in range(1, 4)])
    down_four = jnp.stack([feed_pair[1]] + [along(feed_pair[1], "z", d) for d in range(1, 4)])
    tail_arrived, up_four, down_four, out_block, grad_tokens = lax.optimization_barrier(
        (tail_arrived, up_four, down_four, out_block, grad_tokens)
    )
    up_one, up_three = along(up_four, "z", 1), along(up_four, "z", 3)
    down_one, down_three = along(down_four, "y", 1), along(down_four, "y", 3)
    summed = jnp.sum(tail_arrived.astype(F32), axis=0).astype(BF16)
    slots = summed[:, : 2 * width].reshape(16, 4, 512).transpose(1, 0, 2)
    small = summed[:, 2 * width :].reshape(4, 4, 128)
    crossed = jnp.concatenate([slots, jnp.pad(small, ((0, 0), (0, 12), (0, 0)))], axis=2)
    crossed = lax.all_to_all(crossed, "fsdp", 0, 0, tiled=True)
    mat_qkv = jnp.concatenate([crossed[:, :8, :512], crossed[:, 8:, :part]], axis=2)
    mat_qkv = mat_qkv.reshape(4, 8, 3, part).transpose(1, 2, 0, 3).reshape(8, 3 * width)
    mat_dense = slots[:, 8:, part:].transpose(1, 0, 2).reshape(8, width)
    near = crossed[:, :2, 512:].reshape(4, part)
    vector = jnp.concatenate(
        [
            near.reshape(width),
            jnp.sum(near.astype(F32), axis=0).astype(BF16),
            pick(small, 0, mine)[:2].reshape(part),
            jnp.zeros((2 * part,), BF16),
        ]
    ).reshape(8, part)
    chunk = jnp.concatenate([mat_qkv, mat_dense, vector], axis=1)
    chunk, up_one, up_three, down_one, down_three = lax.optimization_barrier(
        (chunk, up_one, up_three, down_one, down_three)
    )
    tail_full = spread(chunk)
    up_all = [up_four, up_one, along(up_one[:2], "z", 1), along(up_three[2:], "z", 3), up_three]
    down_all = [down_four, down_one, along(down_one[:2], "y", 1), along(down_three[2:], "y", 3), down_three]

    g_up, g_down = local(
        place_kernel,
        jnp.stack([at_y, at_z]),
        [*up_all, *down_all],
        [((part, 4 * width), F32), ((part, 4 * width), F32)],
        [],
        60,
        0,
    )
    vector = tail_full[:, 4 * width :].reshape(blocks, 2 * width).astype(F32)
    g_bqkv = lax.dynamic_slice_in_dim(vector[4:7, :width].reshape(3 * width), mine * 768, 768)
    g_norm = vector[:4, width : width + part]
    g_cot = vector[7, width + part : width + 2 * part]
    g_bup = vector[8:12, width + part : width + 2 * part].reshape(width)
    return (
        out_block.reshape(tokens.shape),
        grad_tokens.reshape(tokens.shape),
        tail_full[:, : 3 * width].astype(F32),
        g_bqkv,
        tail_full[:, 3 * width : 4 * width].astype(F32),
        g_cot,
        g_up,
        g_bup,
        g_down,
        g_cot,
        g_norm[0],
        g_norm[1],
        g_norm[2],
        g_norm[3],
    )


def solution(mesh):
    block = P("ctx", "fsdp", None, None)
    matrix = P("fsdp", None)
    vector = P("fsdp")
    return jax.shard_map(
        on_device,
        mesh=mesh,
        in_specs=(
            block,
            P(),
            matrix,
            vector,
            matrix,
            vector,
            matrix,
            vector,
            matrix,
            vector,
            vector,
            vector,
            vector,
            vector,
            block,
        ),
        out_specs=(
            block,
            block,
            matrix,
            vector,
            matrix,
            vector,
            matrix,
            vector,
            matrix,
            vector,
            vector,
            vector,
            vector,
            vector,
        ),
        check_vma=False,
    )
```

```python
import jax
import jax.numpy as jnp
from jax import lax
from jax.experimental import pallas as pl
from jax.experimental.pallas import tpu as pltpu
from jax.sharding import PartitionSpec as P

HEADS = 16
HEAD_DIM = 64
ROT_DIMS = 16
EPSILON = 1e-05
NEGATIVE = -1e30
F32 = jnp.float32
BF16 = jnp.bfloat16

Q_TILE = 256
K_TILE = 512


def dot(a, b, ca=1, cb=0):
    return lax.dot_general(a, b, (((ca,), (cb,)), ((), ())), preferred_element_type=F32)


def attention_kernel(order_ref, recv_ref, out_ref, kv, kvt, qz, gz, sbuf, dbuf, dkv):
    blocks = recv_ref.shape[0]
    rows = 128
    half_rows = 64
    tiles = blocks * half_rows // Q_TILE
    per_tile = Q_TILE // half_rows
    half = order_ref[blocks]
    lane = lax.broadcasted_iota(jnp.int32, (half_rows, 128), 1)

    def arrange(b, carry):
        c = order_ref[b]
        kv[pl.ds(pl.multiple_of(b * rows, rows), rows), :] = recv_ref[c, 0:rows, :]
        qg = recv_ref[c, rows : rows + half_rows, :].astype(F32)
        at = pl.ds(pl.multiple_of(b * half_rows, half_rows), half_rows)
        qz[at, :] = jnp.where(lane < HEAD_DIM, qg * (HEAD_DIM**-0.5), 0.0).astype(BF16)
        gz[at, :] = jnp.where(lane < HEAD_DIM, 0.0, qg).astype(BF16)
        return carry

    lax.fori_loop(0, blocks, arrange, 0)

    def turn(j, carry):
        at = pl.ds(pl.multiple_of(j * K_TILE, K_TILE), K_TILE)
        kvt[:, at] = kv[at, :].T
        dkv[at, :] = jnp.zeros((K_TILE, 128), F32)
        return carry

    lax.fori_loop(0, tiles, turn, 0)

    key_row = lax.broadcasted_iota(jnp.int32, (K_TILE, Q_TILE), 0)
    query = lax.broadcasted_iota(jnp.int32, (K_TILE, Q_TILE), 1)
    place = (query // half_rows) * rows + half * half_rows + query % half_rows
    allowed = key_row <= place

    def folded(v, op):
        return op(v.reshape(K_TILE // 8, 8, Q_TILE), axis=0)

    def tile(i, carry):
        q_at = pl.ds(pl.multiple_of(i * Q_TILE, Q_TILE), Q_TILE)
        q = qz[q_at, :]
        g = gz[q_at, :]

        def score(j, top):
            at = pl.ds(pl.multiple_of(j * K_TILE, K_TILE), K_TILE)
            s = dot(kv[at, :], q, 1, 1)
            sbuf[at, :] = s
            return jnp.maximum(top, folded(s, jnp.max))

        top = lax.fori_loop(0, i, score, jnp.full((8, Q_TILE), NEGATIVE, F32))
        last = pl.ds(pl.multiple_of(i * K_TILE, K_TILE), K_TILE)
        s = jnp.where(allowed, dot(kv[last, :], q, 1, 1), NEGATIVE)
        sbuf[last, :] = s
        top = jnp.maximum(top, folded(s, jnp.max))
        top = jnp.max(top, axis=0, keepdims=True)

        def weigh(j, carry):
            total, delta = carry
            at = pl.ds(pl.multiple_of(j * K_TILE, K_TILE), K_TILE)
            p = jnp.exp(sbuf[at, :] - top)
            sbuf[at, :] = p
            dp = dot(kv[at, :], g, 1, 1)
            dbuf[at, :] = dp
            return total + folded(p, jnp.sum), delta + folded(p * dp, jnp.sum)

        zero = jnp.zeros((8, Q_TILE), F32)
        total, delta = lax.fori_loop(0, i + 1, weigh, (zero, zero))
        inverse = 1.0 / jnp.sum(total, axis=0, keepdims=True)
        delta = jnp.sum(delta, axis=0, keepdims=True) * inverse

        def spread(j, carry):
            att, dq = carry
            at = pl.ds(pl.multiple_of(j * K_TILE, K_TILE), K_TILE)
            p = sbuf[at, :] * inverse
            pb = p.astype(BF16)
            ds = (p * (dbuf[at, :] - delta)).astype(BF16)
            kt = kvt[:, at]
            dkv[at, :] = dkv[at, :] + (dot(ds, q) + dot(pb, g))
            return att + dot(kt, pb), dq + dot(kt, ds)

        zeros = jnp.zeros((128, Q_TILE), F32)
        att, dq = lax.fori_loop(0, i + 1, spread, (zeros, zeros))
        feature = lax.broadcasted_iota(jnp.int32, (128, Q_TILE), 0)
        both = jnp.where(feature < HEAD_DIM, dq * (HEAD_DIM**-0.5), att).T.astype(BF16)
        for b in range(per_tile):
            c = order_ref[i * per_tile + b]
            out_ref[c, rows : rows + half_rows, :] = both[b * half_rows : (b + 1) * half_rows, :]
        return carry

    lax.fori_loop(0, tiles, tile, 0)

    def put(b, carry):
        c = order_ref[b]
        at = pl.ds(pl.multiple_of(b * rows, rows), rows)
        out_ref[c, 0:rows, :] = dkv[at, :].astype(BF16)
        return carry

    lax.fori_loop(0, blocks, put, 0)


def attention(order, received):
    blocks = received.shape[0]
    keys = blocks * 128
    queries = blocks * 64
    return pl.pallas_call(
        attention_kernel,
        grid_spec=pltpu.PrefetchScalarGridSpec(
            num_scalar_prefetch=1,
            grid=(),
            in_specs=[pl.BlockSpec(memory_space=pltpu.VMEM)],
            out_specs=pl.BlockSpec(memory_space=pltpu.VMEM),
            scratch_shapes=[
                pltpu.VMEM((keys, 128), BF16),
                pltpu.VMEM((128, keys), BF16),
                pltpu.VMEM((queries, 128), BF16),
                pltpu.VMEM((queries, 128), BF16),
                pltpu.VMEM((keys, Q_TILE), F32),
                pltpu.VMEM((keys, Q_TILE), F32),
                pltpu.VMEM((keys, 128), F32),
            ],
        ),
        out_shape=jax.ShapeDtypeStruct(received.shape, BF16),
        compiler_params=pltpu.CompilerParams(vmem_limit_bytes=40 * 1024 * 1024),
        cost_estimate=pl.CostEstimate(
            flops=36 * 10**9, bytes_accessed=2 * received.size * 2, transcendentals=keys * queries // 2
        ),
    )(order, received)


def prepare_kernel(
    ids, x0, x1, x2, x3, w0, w1, w2, w3, w4, w5, w6, dense, cosine, sine_low, sine_high,
    send, low_one, low_two, cots, w_all, vec, bias, proj, att,
):
    rows, part = 128, 256
    natural_weight(ids, (w0, w1, w2, w3, w4, w5, w6), w_all)
    for k, x in enumerate((x0, x1, x2, x3)):
        small = x[rows : rows + 16, :].astype(F32)
        for i in range(6):
            place = slice(part * (i % 4), part * (i % 4 + 1))
            vec[i : i + 1, pl.ds(pl.multiple_of(part * ids[k], part), part)] = small[i // 4 : i // 4 + 1, place]
        for i, place in enumerate(((1, 2), (1, 3), (2, 0))):
            piece = small[place[0] : place[0] + 1, part * place[1] : part * (place[1] + 1)]
            bias[:, pl.ds(pl.multiple_of(768 * ids[k] + part * i, part), part)] = piece
    gone, sone, gtwo, stwo = (vec[i : i + 1, :] for i in range(4))
    for k, x in enumerate((x0, x1, x2, x3)):
        normal, _ = normalise(x[0:rows, :])
        at = slice(k * rows, (k + 1) * rows)
        low_one[at, :] = (normal * gone + sone).astype(BF16)
        low_two[at, :] = (normal * gtwo + stwo).astype(BF16)
    for k, x in enumerate((x0, x1, x2, x3)):
        cots[k * rows : (k + 1) * rows, :] = x[rows + 16 :, :]
    proj[...] = dot(low_one[...], w_all[...])
    att[...] = dot(cots[...], dense[...], 1, 1)
    mine = ids[0]
    biases = [bias[0:1, pl.ds(pl.multiple_of(1024 * i + part * mine, part), part)] for i in range(3)]
    lane = lax.broadcasted_iota(jnp.int32, (rows, 128), 1)
    first = lane < HEAD_DIM
    for k in range(4):
        at = slice(k * rows, (k + 1) * rows)
        qkv = [proj[at, part * i : part * (i + 1)] + biases[i] for i in range(3)]
        query = turned(qkv[0], cosine[...], sine_low[...], sine_high[...])
        key = turned(qkv[1], cosine[...], sine_low[...], sine_high[...])
        grads = att[at, :]
        for p in range(2):
            lanes = slice(128 * p, 128 * (p + 1))
            q, kk, v, a = query[:, lanes], key[:, lanes], qkv[2][:, lanes], grads[:, lanes]
            pairs = (
                (jnp.where(first, kk, pltpu.roll(v, 64, 1)), jnp.where(first, q, pltpu.roll(a, 64, 1))),
                (jnp.where(first, pltpu.roll(kk, 64, 1), v), jnp.where(first, pltpu.roll(q, 64, 1), a)),
            )
            for odd, (kv, qg) in enumerate(pairs):
                base = (4 * k + 2 * p + odd) * 2
                kv, qg = kv.astype(BF16), qg.astype(BF16)
                send[base, 0:128, :] = kv
                send[base + 1, 0:128, :] = kv
                send[base, 128:192, :] = qg[0:64, :]
                send[base + 1, 128:192, :] = qg[64:128, :]


def natural_weight(ids, pieces, whole, lanes=slice(None)):
    own, core, far_two, far_three, *sides = pieces
    for k, piece in ((0, own), (1, core)):
        whole[pl.ds(pl.multiple_of(256 * ids[k], 256), 256), :] = piece[:, lanes]
    for k, piece in ((2, far_two), (3, far_three)):
        start = 256 * ids[k]
        whole[pl.ds(pl.multiple_of(start + 64 * ids[4], 64), 64), :] = piece[:, lanes]
        for n, side in enumerate(sides):
            at = pl.ds(pl.multiple_of(start + 64 * ids[9 + n], 64), 64)
            whole[at, :] = side[64 * (k - 2) : 64 * (k - 1), lanes]


def start_kernel(ids, tokens, cot, weight, v0, v1, v2, v3, v4, v5, v6, packed, own, core, far_two, far_three):
    rows, part = 128, 256
    packed[0:rows, :] = tokens[...]
    packed[rows + 16 :, :] = cot[...]
    vectors = [v[...].astype(F32).reshape(1, v.shape[0]) for v in (v0, v1, v2, v3, v4, v5, v6)]
    zero = jnp.zeros((1, 768), F32)
    lines = [
        jnp.concatenate(vectors[:4], axis=1),
        jnp.concatenate([vectors[4], vectors[5], vectors[6][:, :512]], axis=1),
        jnp.concatenate([vectors[6][:, 512:], zero], axis=1),
        jnp.zeros((13, 4 * part), F32),
    ]
    packed[rows : rows + 16, :] = jnp.concatenate(lines, axis=0).astype(BF16)
    quarter = pl.ds(pl.multiple_of(64 * ids[4], 64), 64)
    for k, piece, at in ((0, own, slice(None)), (1, core, slice(None)), (2, far_two, quarter), (3, far_three, quarter)):
        for i in range(3):
            lanes = pl.ds(pl.multiple_of(1024 * i + part * ids[k], part), part)
            piece[:, part * i : part * (i + 1)] = weight[at, lanes]


def feed_start_kernel(ids, up, down, own, core, far_two, far_three):
    quarter = pl.ds(pl.multiple_of(64 * ids[4], 64), 64)
    for k, piece, at in ((0, own, slice(None)), (1, core, slice(None)), (2, far_two, quarter), (3, far_three, quarter)):
        lanes = pl.ds(pl.multiple_of(1024 * ids[k], 1024), 1024)
        piece[:, 0:1024] = up[at, lanes]
        piece[:, 1024:2048] = down[at, lanes]


def normalise(value):
    value = value.astype(F32)
    centre = value - jnp.mean(value, axis=-1, keepdims=True)
    spread = lax.rsqrt(jnp.mean(centre * centre, axis=-1, keepdims=True) + EPSILON)
    return centre * spread, spread


def turned(u, cosine, sine_low, sine_high):
    halfway = ROT_DIMS // 2
    size = u.shape[1]
    return u * cosine + pltpu.roll(u, size - halfway, 1) * sine_low + pltpu.roll(u, halfway, 1) * sine_high


def feed_kernel(
    ids, low_one, low_two, cots, w0, w1, w2, w3, w4, w5, w6, bias_up,
    by_z, y0, y1, y2, y3, mlp_out, grad_two, sum_up, one_t, up, down, two_t, cots_t,
):
    part = 256
    natural_weight(ids, (w0, w1, w2, w3, w4, w5, w6), up, slice(0, 1024))
    natural_weight(ids, (w0, w1, w2, w3, w4, w5, w6), down, slice(1024, 2048))
    for i in range(4):
        at = slice(part * i, part * (i + 1))
        two_t[at, :] = low_two[:, at].T
        turned_cots = cots[:, at].T
        for x in range(2):
            for y in range(4):
                to = part * ids[i] + 64 * ids[5 + y] + 32 * x
                cots_t[pl.ds(pl.multiple_of(to, 32), 32), :] = turned_cots[128 * x + 32 * y : 128 * x + 32 * y + 32, :]
        one_t[at, :] = low_one[:, at].T
    for i in range(4):
        at = slice(part * i, part * (i + 1))
        pre = dot(low_two[...], up[:, at]) + bias_up[0:1, at]
        cdf = 0.5 * (1.0 + lax.erf(pre * (0.5**0.5)))
        slope = cdf + pre * (jnp.exp(-0.5 * pre * pre) * 0.3989422804014327)
        act = (pre * cdf).astype(BF16)
        grad = (dot(cots[...], down[:, at]) * slope).astype(BF16)
        out = dot(act, down[:, at], 1, 1)
        back = dot(grad, up[:, at], 1, 1)
        if i == 0:
            mlp_out[...] = out
            grad_two[...] = back
        else:
            mlp_out[...] = mlp_out[...] + out
            grad_two[...] = grad_two[...] + back
        sum_up[:, at] = jnp.sum(grad.astype(F32).reshape(64, 8, part), axis=0)
        for pair in range(2):
            gup, gdown = [], []
            for k in (2 * pair, 2 * pair + 1):
                owner = pl.ds(pl.multiple_of(part * ids[k], part), part)
                gup.append(dot(two_t[owner, :], grad).reshape(2, 4, 4, 8, part))
                gdown.append(dot(cots_t[part * k : part * (k + 1), :], act).reshape(4, 8, 8, part))
            for n in range(4):
                piece = jnp.concatenate([v[:, :, n] for v in gup], axis=2).reshape(8, 16, part)
                by_z[n, :, pair, :, at] = piece.astype(BF16)
                piece = jnp.concatenate([v[n] for v in gdown], axis=1)
                (y0, y1, y2, y3)[n][:, pair, :, at] = piece.astype(BF16)


def finish_kernel(
    ids, back, w_all, dense, x0, x1, x2, x3, vec, cosine, sine_low, sine_high, one_t, cots, mlp_out, grad_two, sum_up,
    message, own_part, sent, sent_far, grads, att, g_one, sums, dense_grad,
):
    rows, part = 128, 256
    lane = lax.broadcasted_iota(jnp.int32, (rows, 128), 1)
    first = lane < HEAD_DIM
    for k in range(4):
        at = slice(k * rows, (k + 1) * rows)
        pieces = [[], [], [], []]
        for p in range(2):
            kvs, qas = [], []
            for odd in range(2):
                base = (4 * k + 2 * p + odd) * 2
                kvs.append(back[base, 0:128, :].astype(F32) + back[base + 1, 0:128, :].astype(F32))
                qas.append(
                    jnp.concatenate([back[base, 128:192, :].astype(F32), back[base + 1, 128:192, :].astype(F32)], axis=0)
                )
            for into, pair in ((pieces[1], kvs), (pieces[0], qas)):
                into.append(jnp.where(first, pair[0], pltpu.roll(pair[1], 64, 1)))
            for into, pair in ((pieces[2], kvs), (pieces[3], qas)):
                into.append(jnp.where(first, pltpu.roll(pair[0], 64, 1), pair[1]))
        dq, dk, dv, out = (jnp.concatenate(piece, axis=1) for piece in pieces)
        dq = turned(dq, cosine[...], -sine_low[...], -sine_high[...])
        dk = turned(dk, cosine[...], -sine_low[...], -sine_high[...])
        grads[at, 0:part] = dq.astype(BF16)
        grads[at, part : 2 * part] = dk.astype(BF16)
        grads[at, 2 * part :] = dv.astype(BF16)
        att[at, :] = out.astype(BF16)
    dense_grad[...] = dot(att[...], cots[...], 0, 0).reshape(32, 8, 4 * part)
    for k in range(4):
        owner = pl.ds(pl.multiple_of(part * ids[k], part), part)
        gqkv = dot(one_t[owner, :], grads[...]).reshape(32, 8, 3 * part)
        lower = jnp.concatenate([gqkv[:, :, 512:], dense_grad[:, :, owner]], axis=2)
        message[:, :, pl.ds(pl.multiple_of(512 * ids[k], 512), 512)] = jnp.concatenate([gqkv[:, :, :512], lower], axis=1).astype(BF16)
    g_one[...] = dot(grads[...], w_all[...], 1, 1)
    gone, gtwo = vec[0:1, :], vec[2:3, :]
    biases = vec[4:5, :] + vec[5:6, :]
    folded = [jnp.zeros((8, 4 * part), F32) for _ in range(5)]
    for k, x in enumerate((x0, x1, x2, x3)):
        at = slice(k * rows, (k + 1) * rows)
        normal, spread = normalise(x[0:rows, :])
        one, two = g_one[at, :], grad_two[at, :]
        cot = cots[at, :].astype(F32)
        for i, value in enumerate((one * normal, one, two * normal, two, cot)):
            folded[i] = folded[i] + jnp.sum(value.reshape(16, 8, 4 * part), axis=0)
        e = one * gone + two * gtwo
        inner = spread * (
            e - jnp.mean(e, axis=-1, keepdims=True) - normal * jnp.mean(e * normal, axis=-1, keepdims=True)
        )
        outer = mlp_out[at, :] + dot(att[at, :], dense[...])
        if k == 0:
            own_part[:, 0 : 4 * part] = outer + x[0:rows, :].astype(F32) + biases
            own_part[:, 4 * part :] = inner + cot
        else:
            into = sent_far if k == 2 else sent.at[k // 2]
            into[:, 0 : 4 * part] = outer.astype(BF16)
            into[:, 4 * part :] = inner.astype(BF16)
    row = lax.broadcasted_iota(jnp.int32, (16, 128), 0)

    def put(v, values):
        block = jnp.zeros((16, 128), F32)
        for k, value in enumerate(values):
            block = jnp.where(row == 4 * ids[k], value[:, 0:128], block)
            block = jnp.where(row == 4 * ids[k] + 1, value[:, 128:256], block)
        message[v, :, 2048:2176] = block.astype(BF16)

    sums[...] = jnp.zeros_like(sums)
    for i in range(5):
        sums[i : i + 1, :] = jnp.sum(folded[i], axis=0, keepdims=True)
    message[:, :, 2048:2176] = jnp.zeros((32, 16, 128), BF16)
    total = jnp.sum(grads[...].astype(F32), axis=0, keepdims=True)
    ups = jnp.sum(sum_up[...], axis=0, keepdims=True)
    owners = [pl.ds(pl.multiple_of(part * ids[k], part), part) for k in range(4)]
    for v in range(4):
        put(v, [sums[v : v + 1, owner] for owner in owners])
    for v in range(3):
        put(4 + v, [total[:, part * v : part * (v + 1)]] * 4)
    put(7, [sums[4:5, owner] for owner in owners])
    for v in range(4):
        put(8 + v, [ups[:, part * v : part * (v + 1)]] * 4)


def place_kernel(
    ids, u0, u1, u2, v2, u3, d0, d1, d2, e2, d3, tail, up, down, qkv, dense,
    up_rows, down_rows, qkv_rows, dense_rows, sems,
):
    width = 2048
    copies = []

    def send(rows, out, n):
        copies.append(pltpu.make_async_copy(rows, out, sems.at[n]))
        copies[-1].start()

    def put(piece, into):
        value = piece.astype(F32)
        into[:, 0:width] = value[0:8, :]
        into[:, width:] = value[8:16, :]

    for d, (one, two) in enumerate(((u0, d0), (u1, d1), (u3, d3), ((u2, v2), (d2, e2)))):
        steps = (0, 1, 3, 2)[d]
        for e in range(4):
            near_y, near_z = lax.rem(ids[0] + 4 - e, 4), lax.rem(ids[1] + 4 - e, 4)
            for x in range(2):
                if steps == 2:
                    piece_one, piece_two = one[e // 2][e % 2, x], two[e // 2][e % 2, x]
                else:
                    piece_one, piece_two = one[e, x], two[e, x]
                put(piece_one, up_rows.at[d, 4 * x + near_y])
                put(piece_two, down_rows.at[d, x, near_z])
        send(up_rows.at[d], up.at[:, lax.rem(ids[1] + 4 - steps, 4)], 2 * d)
        send(down_rows.at[d], down.at[:, lax.rem(ids[0] + 4 - steps, 4)], 2 * d + 1)
    qkv_rows[...] = tail[:, 0:3072].astype(F32)
    send(qkv_rows, qkv, 8)
    dense_rows[...] = tail[:, 3072:4096].astype(F32)
    send(dense_rows, dense, 9)
    for copy in copies:
        copy.wait()


def local(kernel, ids, inputs, outs, scratch, limit, micros, space=pltpu.VMEM):
    shapes = [jax.ShapeDtypeStruct(shape, dtype) for shape, dtype in outs]
    moved = sum(v.size * v.dtype.itemsize for v in list(inputs) + shapes)
    return pl.pallas_call(
        kernel,
        grid_spec=pltpu.PrefetchScalarGridSpec(
            num_scalar_prefetch=1,
            grid=(),
            in_specs=[pl.BlockSpec(memory_space=pltpu.VMEM)] * len(inputs),
            out_specs=[pl.BlockSpec(memory_space=space)] * len(outs),
            scratch_shapes=[pltpu.VMEM(*item) if item else pltpu.SemaphoreType.DMA((10,)) for item in scratch],
        ),
        out_shape=shapes,
        compiler_params=pltpu.CompilerParams(vmem_limit_bytes=limit * 1024 * 1024),
        cost_estimate=pl.CostEstimate(flops=micros * 10**9, bytes_accessed=moved, transcendentals=0),
    )(ids, *inputs)


def swap(value, flip):
    return lax.ppermute(value, "fsdp", [(i, i ^ flip) for i in range(4)])


def across(value, flip_ctx, flip):
    order = [(4 * c + f, 4 * (c ^ flip_ctx) + (f ^ flip)) for c in range(32) for f in range(4)]
    return lax.ppermute(value, ("ctx", "fsdp"), order)


def along(value, steps_y, steps_z):
    order = []
    for c in range(32):
        x, y, z = c // 16, (c // 4) % 4, c % 4
        order.append((c, 16 * x + 4 * ((y + steps_y) % 4) + (z + steps_z) % 4))
    return lax.ppermute(value, "ctx", order)


def flipped(value, flip):
    return lax.ppermute(value, "ctx", [(c, c ^ flip) for c in range(32)])


def beside(far):
    both = jnp.concatenate(far)
    return [along(both, 1, 0), along(both, 0, 1), along(both, -1, -1)]


def on_device(
    tokens,
    block_order,
    weight_qkv,
    bias_qkv,
    weight_dense,
    bias_dense,
    weight_up,
    bias_up,
    weight_down,
    bias_down,
    gain_one,
    shift_one,
    gain_two,
    shift_two,
    cotangent,
):
    rows = tokens.shape[2]
    width = tokens.shape[3]
    blocks = lax.axis_size("ctx")
    ctx = lax.axis_index("ctx").astype(jnp.int32)
    mine = lax.axis_index("fsdp").astype(jnp.int32)
    part = width // 4
    at_x, at_y, at_z = ctx // 16, (ctx // 4) % 4, ctx % 4
    quarter = 2 * (at_y % 2) + at_z % 2
    ids = jnp.stack([mine, mine ^ 1, mine ^ 2, mine ^ 3, quarter] + [(n - at_y) % 4 for n in range(4)] + [quarter ^ 2, quarter ^ 1, quarter ^ 3])
    own_tokens = tokens.reshape(rows, width)
    own_cot = cotangent.reshape(rows, width)

    def gather(value):
        over = swap(value, 2)
        return [value, swap(value, 1), over, swap(over, 1)]

    packed, qkv_own, qkv_core, *qkv_far = local(
        start_kernel,
        ids,
        [
            own_tokens, own_cot, weight_qkv,
            gain_one, shift_one, gain_two, shift_two, bias_dense, bias_down, bias_qkv,
        ],
        [((272, width), BF16), ((part, 768), BF16), ((part, 768), BF16), ((64, 768), BF16), ((64, 768), BF16)],
        [],
        60,
        4,
    )
    feed_own, feed_core, *feed_far = local(
        feed_start_kernel,
        ids,
        [weight_up, weight_down],
        [((part, 2 * width), BF16)] * 2 + [((64, 2 * width), BF16)] * 2,
        [],
        60,
        5,
    )
    qkv_far = [across(piece, 16, k) for k, piece in zip((2, 3), qkv_far)]
    packed = gather(packed)
    feed_far, qkv_far, packed[2] = lax.optimization_barrier((feed_far, qkv_far, packed[2]))
    qkv_pieces = [qkv_own, swap(qkv_core, 1), *qkv_far, *beside(qkv_far)]
    feed_far = [across(piece, 16, k) for k, piece in zip((2, 3), feed_far)]
    feed_core = swap(feed_core, 1)

    places = (block_order[ctx] * rows + lax.broadcasted_iota(jnp.int32, (rows, part), 0)).astype(F32)
    lane = lax.broadcasted_iota(jnp.int32, (rows, part), 1) % HEAD_DIM
    halfway = ROT_DIMS // 2
    inverse = 10000.0 ** (-2.0 * (lane % halfway).astype(F32) / ROT_DIMS)
    phases = jnp.where(lane < ROT_DIMS, places * inverse, 0.0)
    sines = jnp.sin(phases)
    tables = [
        jnp.cos(phases),
        jnp.where(lane < halfway, -sines, 0.0),
        jnp.where(lane < halfway, 0.0, sines),
    ]

    message, low_one, low_two, four_cot, my_qkv, vec = local(
        prepare_kernel,
        ids,
        [*packed, *qkv_pieces, weight_dense, *tables],
        [
            ((blocks, 192, 128), BF16),
            ((4 * rows, width), BF16),
            ((4 * rows, width), BF16),
            ((4 * rows, width), BF16),
            ((width, 3 * part), BF16),
            ((8, width), F32),
        ],
        [((1, 3 * width), F32), ((4 * rows, 3 * part), F32), ((4 * rows, part), F32)],
        60,
        7,
    )
    message, feed_far = lax.optimization_barrier((message, feed_far))
    feed_pieces = [feed_own, feed_core, *feed_far, *beside(feed_far)]
    message, feed_pieces = lax.optimization_barrier((message, feed_pieces))
    received = lax.all_to_all(message, "ctx", 0, 0, tiled=True)
    order = jnp.zeros((blocks,), jnp.int32).at[block_order].set(jnp.arange(blocks, dtype=jnp.int32))
    order = jnp.concatenate([order, (ctx % 2)[None]])

    by_z, y0, y1, y2, y3, mlp_out, grad_two, sum_up, one_t = local(
        feed_kernel,
        ids,
        [low_one, low_two, four_cot, *feed_pieces, bias_up.astype(F32).reshape(1, width)],
        [
            ((4, 8, 2, 16, width), BF16),
            ((8, 2, 16, width), BF16),
            ((8, 2, 16, width), BF16),
            ((8, 2, 16, width), BF16),
            ((8, 2, 16, width), BF16),
            ((4 * rows, width), F32),
            ((4 * rows, width), F32),
            ((8, width), F32),
            ((width, 4 * rows), BF16),
        ],
        [((width, width), BF16), ((width, width), BF16), ((width, 4 * rows), BF16), ((width, 4 * rows), BF16)],
        60,
        14,
    )
    natural = jnp.arange(4) ^ mine

    def spread(chunk):
        copies = jnp.broadcast_to(chunk[None], (blocks,) + chunk.shape)
        return lax.all_to_all(copies, "ctx", 0, 0, tiled=True).reshape(blocks * chunk.shape[0], chunk.shape[1])

    def added(pieces):
        total = pieces[0].astype(F32)
        for piece in pieces[1:]:
            total = total + piece.astype(F32)
        return total.astype(BF16)

    def pick(value, axis, n):
        return lax.dynamic_index_in_dim(value, n, axis, keepdims=False)

    groups = [[4 * n + z for z in range(4)] for n in range(8)]
    up_in = lax.all_to_all(by_z, "ctx", 0, 0, tiled=True, axis_index_groups=groups)
    down_in = [y0] + [along(y, d + 1, 0) for d, y in enumerate((y1, y2, y3))]
    answer = attention(order, received)
    answer, up_in, down_in = lax.optimization_barrier((answer, up_in, down_in))
    up_sum = added([up_in[n] for n in range(4)]).reshape(2, 4, 2, 16, width)
    down_sum = added(down_in).reshape(2, 4, 2, 16, width)

    up_in = [pick(up_sum, 1, at_y)] + [along(pick(up_sum, 1, (at_y + d) % 4), d, 0) for d in range(1, 4)]
    down_in = [pick(down_sum, 1, at_z)] + [along(pick(down_sum, 1, (at_z + d) % 4), 0, d) for d in range(1, 4)]
    back = lax.all_to_all(answer, "ctx", 0, 0, tiled=True)
    back, up_in, down_in = lax.optimization_barrier((back, up_in, down_in))
    feed_sum = jnp.stack([added(up_in), added(down_in)], axis=1)
    feed_slots = feed_sum.reshape(2, 2, 4, 8, width)
    feed_cross = [feed_slots[:, :, 0]] + [swap(feed_slots[:, :, k], k) for k in range(1, 4)]
    feed_cross = jnp.stack(feed_cross)[natural]

    tail, own_part, sent, sent_far = local(
        finish_kernel,
        ids,
        [back, my_qkv, weight_dense, *packed, vec, *tables, one_t, four_cot, mlp_out, grad_two, sum_up],
        [((blocks, 16, 2176), BF16), ((rows, 2 * width), F32), ((2, rows, 2 * width), BF16), ((rows, 2 * width), BF16)],
        [((4 * rows, 3 * part), BF16), ((4 * rows, part), BF16), ((4 * rows, width), F32), ((8, width), F32), ((32, 8, width), F32)],
        60,
        12,
    )
    tail, feed_cross = lax.optimization_barrier((tail, feed_cross))
    feed_pair = added([feed_cross, across(feed_cross, 16, 0)]).reshape(2, 2, 2, 2, 8, width)
    feed_pair = feed_pair.transpose(3, 2, 0, 4, 1, 5).reshape(2, 2, 16, 2 * width)
    tail_arrived = lax.all_to_all(tail, "ctx", 0, 0, tiled=True)

    near = swap(sent, 1).astype(F32)
    both = own_part + near[0] + swap((sent_far.astype(F32) + near[1]).astype(BF16), 2).astype(F32)
    out_block, grad_tokens = both[:, :width].astype(BF16), both[:, width:].astype(BF16)

    up_four = jnp.stack([feed_pair[0]] + [along(feed_pair[0], d, 0) for d in range(1, 4)])
    down_four = jnp.stack([feed_pair[1]] + [along(feed_pair[1], 0, d) for d in range(1, 4)])
    tail_arrived, up_four, down_four, out_block, grad_tokens = lax.optimization_barrier(
        (tail_arrived, up_four, down_four, out_block, grad_tokens)
    )
    up_one, up_three = along(up_four, 0, 1), along(up_four, 0, 3)
    down_one, down_three = along(down_four, 1, 0), along(down_four, 3, 0)
    summed = jnp.sum(tail_arrived.astype(F32), axis=0).astype(BF16)
    slots = summed[:, : 2 * width].reshape(16, 4, 512).transpose(1, 0, 2)
    small = summed[:, 2 * width :].reshape(4, 4, 128)
    crossed = jnp.concatenate([slots, jnp.pad(small, ((0, 0), (0, 12), (0, 0)))], axis=2)
    crossed = lax.all_to_all(crossed, "fsdp", 0, 0, tiled=True)
    mat_qkv = jnp.concatenate([crossed[:, :8, :512], crossed[:, 8:, :part]], axis=2)
    mat_qkv = mat_qkv.reshape(4, 8, 3, part).transpose(1, 2, 0, 3).reshape(8, 3 * width)
    mat_dense = slots[:, 8:, part:].transpose(1, 0, 2).reshape(8, width)
    near = crossed[:, :2, 512:].reshape(4, part)
    vector = jnp.concatenate(
        [
            near.reshape(width),
            jnp.sum(near.astype(F32), axis=0).astype(BF16),
            pick(small, 0, mine)[:2].reshape(part),
            jnp.zeros((2 * part,), BF16),
        ]
    ).reshape(8, part)
    chunk = jnp.concatenate([mat_qkv, mat_dense, vector], axis=1)
    chunk, up_one, up_three, down_one, down_three = lax.optimization_barrier(
        (chunk, up_one, up_three, down_one, down_three)
    )
    tail_full = spread(chunk)
    up_all = [up_four, up_one, along(up_one[:2], 0, 1), along(up_three[2:], 0, 3), up_three]
    down_all = [down_four, down_one, along(down_one[:2], 1, 0), along(down_three[2:], 3, 0), down_three]

    g_up, g_down, g_qkv, g_dense = local(
        place_kernel,
        jnp.stack([at_y, at_z]),
        [*up_all, *down_all, tail_full],
        [((8, 4, 8, 4 * width), F32), ((2, 4, 4, 8, 4 * width), F32), ((part, 3 * width), F32), ((part, width), F32)],
        [
            ((4, 8, 8, 4 * width), F32),
            ((4, 2, 4, 8, 4 * width), F32),
            ((part, 3 * width), F32),
            ((part, width), F32),
            None,
        ],
        60,
        6,
        pl.ANY,
    )
    g_up, g_down = g_up.reshape(part, 4 * width), g_down.reshape(part, 4 * width)
    vector = tail_full[:, 4 * width :].reshape(blocks, 2 * width).astype(F32)
    g_bqkv = lax.dynamic_slice_in_dim(vector[4:7, :width].reshape(3 * width), mine * 768, 768)
    g_norm = vector[:4, width : width + part]
    g_cot = vector[7, width + part : width + 2 * part]
    g_bup = vector[8:12, width + part : width + 2 * part].reshape(width)
    return (
        out_block.reshape(tokens.shape),
        grad_tokens.reshape(tokens.shape),
        g_qkv,
        g_bqkv,
        g_dense,
        g_cot,
        g_up,
        g_bup,
        g_down,
        g_cot,
        g_norm[0],
        g_norm[1],
        g_norm[2],
        g_norm[3],
    )


def solution(mesh):
    block = P("ctx", "fsdp", None, None)
    matrix = P("fsdp", None)
    vector = P("fsdp")
    return jax.shard_map(
        on_device,
        mesh=mesh,
        in_specs=(
            block,
            P(),
            matrix,
            vector,
            matrix,
            vector,
            matrix,
            vector,
            matrix,
            vector,
            vector,
            vector,
            vector,
            vector,
            block,
        ),
        out_specs=(
            block,
            block,
            matrix,
            vector,
            matrix,
            vector,
            matrix,
            vector,
            matrix,
            vector,
            vector,
            vector,
            vector,
            vector,
        ),
        check_vma=False,
    )
```

```python
import jax
import jax.numpy as jnp
from jax import lax
from jax.experimental import pallas as pl
from jax.experimental.pallas import tpu as pltpu
from jax.sharding import PartitionSpec as P

HEADS = 16
HEAD_DIM = 64
ROT_DIMS = 16
EPSILON = 1e-05
NEGATIVE = -1e30
F32 = jnp.float32
BF16 = jnp.bfloat16

Q_TILE = 256
K_TILE = 512


def dot(a, b, ca=1, cb=0):
    return lax.dot_general(a, b, (((ca,), (cb,)), ((), ())), preferred_element_type=F32)


def attention_kernel(order_ref, recv_ref, out_ref, kv, kvt, qz, gz, sbuf, dbuf, dkv):
    blocks = recv_ref.shape[0]
    rows = 128
    half_rows = 64
    tiles = blocks * half_rows // Q_TILE
    per_tile = Q_TILE // half_rows
    half = order_ref[blocks]
    lane = lax.broadcasted_iota(jnp.int32, (half_rows, 128), 1)

    def arrange(b, carry):
        c = order_ref[b]
        kv[pl.ds(pl.multiple_of(b * rows, rows), rows), :] = recv_ref[c, 0:rows, :]
        qg = recv_ref[c, rows : rows + half_rows, :].astype(F32)
        at = pl.ds(pl.multiple_of(b * half_rows, half_rows), half_rows)
        qz[at, :] = jnp.where(lane < HEAD_DIM, qg * (HEAD_DIM**-0.5), 0.0).astype(BF16)
        gz[at, :] = jnp.where(lane < HEAD_DIM, 0.0, qg).astype(BF16)
        return carry

    lax.fori_loop(0, blocks, arrange, 0)

    def turn(j, carry):
        at = pl.ds(pl.multiple_of(j * K_TILE, K_TILE), K_TILE)
        kvt[:, at] = kv[at, :].T
        dkv[at, :] = jnp.zeros((K_TILE, 128), F32)
        return carry

    lax.fori_loop(0, tiles, turn, 0)

    key_row = lax.broadcasted_iota(jnp.int32, (K_TILE, Q_TILE), 0)
    query = lax.broadcasted_iota(jnp.int32, (K_TILE, Q_TILE), 1)
    place = (query // half_rows) * rows + half * half_rows + query % half_rows
    allowed = key_row <= place

    def folded(v, op):
        return op(v.reshape(K_TILE // 8, 8, Q_TILE), axis=0)

    def tile(i, carry):
        q_at = pl.ds(pl.multiple_of(i * Q_TILE, Q_TILE), Q_TILE)
        q = qz[q_at, :]
        g = gz[q_at, :]

        def score(j, top):
            at = pl.ds(pl.multiple_of(j * K_TILE, K_TILE), K_TILE)
            s = dot(kv[at, :], q, 1, 1)
            sbuf[at, :] = s
            return jnp.maximum(top, folded(s, jnp.max))

        top = lax.fori_loop(0, i, score, jnp.full((8, Q_TILE), NEGATIVE, F32))
        last = pl.ds(pl.multiple_of(i * K_TILE, K_TILE), K_TILE)
        s = jnp.where(allowed, dot(kv[last, :], q, 1, 1), NEGATIVE)
        sbuf[last, :] = s
        top = jnp.maximum(top, folded(s, jnp.max))
        top = jnp.max(top, axis=0, keepdims=True)

        def weigh(j, carry):
            total, delta = carry
            at = pl.ds(pl.multiple_of(j * K_TILE, K_TILE), K_TILE)
            p = jnp.exp(sbuf[at, :] - top)
            sbuf[at, :] = p
            dp = dot(kv[at, :], g, 1, 1)
            dbuf[at, :] = dp
            return total + folded(p, jnp.sum), delta + folded(p * dp, jnp.sum)

        zero = jnp.zeros((8, Q_TILE), F32)
        total, delta = lax.fori_loop(0, i + 1, weigh, (zero, zero))
        inverse = 1.0 / jnp.sum(total, axis=0, keepdims=True)
        delta = jnp.sum(delta, axis=0, keepdims=True) * inverse

        def spread(j, carry):
            att, dq = carry
            at = pl.ds(pl.multiple_of(j * K_TILE, K_TILE), K_TILE)
            p = sbuf[at, :] * inverse
            pb = p.astype(BF16)
            ds = (p * (dbuf[at, :] - delta)).astype(BF16)
            kt = kvt[:, at]
            dkv[at, :] = dkv[at, :] + (dot(ds, q) + dot(pb, g))
            return att + dot(kt, pb), dq + dot(kt, ds)

        zeros = jnp.zeros((128, Q_TILE), F32)
        att, dq = lax.fori_loop(0, i + 1, spread, (zeros, zeros))
        feature = lax.broadcasted_iota(jnp.int32, (128, Q_TILE), 0)
        both = jnp.where(feature < HEAD_DIM, dq * (HEAD_DIM**-0.5), att).T.astype(BF16)
        for b in range(per_tile):
            c = order_ref[i * per_tile + b]
            out_ref[c, rows : rows + half_rows, :] = both[b * half_rows : (b + 1) * half_rows, :]
        return carry

    lax.fori_loop(0, tiles, tile, 0)

    def put(b, carry):
        c = order_ref[b]
        at = pl.ds(pl.multiple_of(b * rows, rows), rows)
        out_ref[c, 0:rows, :] = dkv[at, :].astype(BF16)
        return carry

    lax.fori_loop(0, blocks, put, 0)


def attention(order, received):
    blocks = received.shape[0]
    keys = blocks * 128
    queries = blocks * 64
    return pl.pallas_call(
        attention_kernel,
        grid_spec=pltpu.PrefetchScalarGridSpec(
            num_scalar_prefetch=1,
            grid=(),
            in_specs=[pl.BlockSpec(memory_space=pltpu.VMEM)],
            out_specs=pl.BlockSpec(memory_space=pltpu.VMEM),
            scratch_shapes=[
                pltpu.VMEM((keys, 128), BF16),
                pltpu.VMEM((128, keys), BF16),
                pltpu.VMEM((queries, 128), BF16),
                pltpu.VMEM((queries, 128), BF16),
                pltpu.VMEM((keys, Q_TILE), F32),
                pltpu.VMEM((keys, Q_TILE), F32),
                pltpu.VMEM((keys, 128), F32),
            ],
        ),
        out_shape=jax.ShapeDtypeStruct(received.shape, BF16),
        compiler_params=pltpu.CompilerParams(vmem_limit_bytes=40 * 1024 * 1024),
        cost_estimate=pl.CostEstimate(
            flops=36 * 10**9, bytes_accessed=2 * received.size * 2, transcendentals=keys * queries // 2
        ),
    )(order, received)


def prepare_kernel(
    ids, x0, x1, x2, x3, w0, w1, w2, w3, w4, w5, w6, dense, cosine, sine_low, sine_high,
    send, low_one, low_two, cots, w_all, vec, bias, proj, att,
):
    rows, part = 128, 256
    natural_weight(ids, (w0, w1, w2, w3, w4, w5, w6), w_all)
    for k, x in enumerate((x0, x1, x2, x3)):
        small = x[rows : rows + 16, :].astype(F32)
        for i in range(6):
            place = slice(part * (i % 4), part * (i % 4 + 1))
            vec[i : i + 1, pl.ds(pl.multiple_of(part * ids[k], part), part)] = small[i // 4 : i // 4 + 1, place]
        for i, place in enumerate(((1, 2), (1, 3), (2, 0))):
            piece = small[place[0] : place[0] + 1, part * place[1] : part * (place[1] + 1)]
            bias[:, pl.ds(pl.multiple_of(768 * ids[k] + part * i, part), part)] = piece
    gone, sone, gtwo, stwo = (vec[i : i + 1, :] for i in range(4))
    for k, x in enumerate((x0, x1, x2, x3)):
        normal, _ = normalise(x[0:rows, :])
        at = slice(k * rows, (k + 1) * rows)
        low_one[at, :] = (normal * gone + sone).astype(BF16)
        low_two[at, :] = (normal * gtwo + stwo).astype(BF16)
    for k, x in enumerate((x0, x1, x2, x3)):
        cots[k * rows : (k + 1) * rows, :] = x[rows + 16 :, :]
    proj[...] = dot(low_one[...], w_all[...])
    att[...] = dot(cots[...], dense[...], 1, 1)
    mine = ids[0]
    biases = [bias[0:1, pl.ds(pl.multiple_of(1024 * i + part * mine, part), part)] for i in range(3)]
    lane = lax.broadcasted_iota(jnp.int32, (rows, 128), 1)
    first = lane < HEAD_DIM
    for k in range(4):
        at = slice(k * rows, (k + 1) * rows)
        qkv = [proj[at, part * i : part * (i + 1)] + biases[i] for i in range(3)]
        query = turned(qkv[0], cosine[...], sine_low[...], sine_high[...])
        key = turned(qkv[1], cosine[...], sine_low[...], sine_high[...])
        grads = att[at, :]
        for p in range(2):
            lanes = slice(128 * p, 128 * (p + 1))
            q, kk, v, a = query[:, lanes], key[:, lanes], qkv[2][:, lanes], grads[:, lanes]
            pairs = (
                (jnp.where(first, kk, pltpu.roll(v, 64, 1)), jnp.where(first, q, pltpu.roll(a, 64, 1))),
                (jnp.where(first, pltpu.roll(kk, 64, 1), v), jnp.where(first, pltpu.roll(q, 64, 1), a)),
            )
            for odd, (kv, qg) in enumerate(pairs):
                base = (4 * k + 2 * p + odd) * 2
                kv, qg = kv.astype(BF16), qg.astype(BF16)
                send[base, 0:128, :] = kv
                send[base + 1, 0:128, :] = kv
                send[base, 128:192, :] = qg[0:64, :]
                send[base + 1, 128:192, :] = qg[64:128, :]


def natural_weight(ids, pieces, whole, lanes=slice(None)):
    own, core, far_two, far_three, *sides = pieces
    for k, piece in ((0, own), (1, core)):
        whole[pl.ds(pl.multiple_of(256 * ids[k], 256), 256), :] = piece[:, lanes]
    for k, piece in ((2, far_two), (3, far_three)):
        start = 256 * ids[k]
        whole[pl.ds(pl.multiple_of(start + 64 * ids[4], 64), 64), :] = piece[:, lanes]
        for n, side in enumerate(sides):
            at = pl.ds(pl.multiple_of(start + 64 * ids[9 + n], 64), 64)
            whole[at, :] = side[64 * (k - 2) : 64 * (k - 1), lanes]


def start_kernel(ids, tokens, cot, weight, v0, v1, v2, v3, v4, v5, v6, packed, own, core, far_two, far_three):
    rows, part = 128, 256
    packed[0:rows, :] = tokens[...]
    packed[rows + 16 :, :] = cot[...]
    vectors = [v[...].astype(F32).reshape(1, v.shape[0]) for v in (v0, v1, v2, v3, v4, v5, v6)]
    zero = jnp.zeros((1, 768), F32)
    lines = [
        jnp.concatenate(vectors[:4], axis=1),
        jnp.concatenate([vectors[4], vectors[5], vectors[6][:, :512]], axis=1),
        jnp.concatenate([vectors[6][:, 512:], zero], axis=1),
        jnp.zeros((13, 4 * part), F32),
    ]
    packed[rows : rows + 16, :] = jnp.concatenate(lines, axis=0).astype(BF16)
    quarter = pl.ds(pl.multiple_of(64 * ids[4], 64), 64)
    for k, piece, at in ((0, own, slice(None)), (1, core, slice(None)), (2, far_two, quarter), (3, far_three, quarter)):
        for i in range(3):
            lanes = pl.ds(pl.multiple_of(1024 * i + part * ids[k], part), part)
            piece[:, part * i : part * (i + 1)] = weight[at, lanes]


def feed_start_kernel(ids, up, down, own, core, far_two, far_three):
    quarter = pl.ds(pl.multiple_of(64 * ids[4], 64), 64)
    for k, piece, at in ((0, own, slice(None)), (1, core, slice(None)), (2, far_two, quarter), (3, far_three, quarter)):
        lanes = pl.ds(pl.multiple_of(1024 * ids[k], 1024), 1024)
        piece[:, 0:1024] = up[at, lanes]
        piece[:, 1024:2048] = down[at, lanes]


def normalise(value):
    value = value.astype(F32)
    centre = value - jnp.mean(value, axis=-1, keepdims=True)
    spread = lax.rsqrt(jnp.mean(centre * centre, axis=-1, keepdims=True) + EPSILON)
    return centre * spread, spread


def turned(u, cosine, sine_low, sine_high):
    halfway = ROT_DIMS // 2
    size = u.shape[1]
    return u * cosine + pltpu.roll(u, size - halfway, 1) * sine_low + pltpu.roll(u, halfway, 1) * sine_high


def feed_kernel(
    ids, low_one, low_two, cots, w0, w1, w2, w3, w4, w5, w6, bias_up,
    by_z, y0, y1, y2, y3, mlp_out, grad_two, sum_up, one_t, up, down, two_t, cots_t,
):
    part = 256
    natural_weight(ids, (w0, w1, w2, w3, w4, w5, w6), up, slice(0, 1024))
    natural_weight(ids, (w0, w1, w2, w3, w4, w5, w6), down, slice(1024, 2048))
    for i in range(4):
        at = slice(part * i, part * (i + 1))
        two_t[at, :] = low_two[:, at].T
        turned_cots = cots[:, at].T
        for x in range(2):
            for y in range(4):
                to = part * ids[i] + 64 * ids[5 + y] + 32 * x
                cots_t[pl.ds(pl.multiple_of(to, 32), 32), :] = turned_cots[128 * x + 32 * y : 128 * x + 32 * y + 32, :]
        one_t[at, :] = low_one[:, at].T
    for i in range(4):
        at = slice(part * i, part * (i + 1))
        pre = dot(low_two[...], up[:, at]) + bias_up[0:1, at]
        cdf = 0.5 * (1.0 + lax.erf(pre * (0.5**0.5)))
        slope = cdf + pre * (jnp.exp(-0.5 * pre * pre) * 0.3989422804014327)
        act = (pre * cdf).astype(BF16)
        grad = (dot(cots[...], down[:, at]) * slope).astype(BF16)
        out = dot(act, down[:, at], 1, 1)
        back = dot(grad, up[:, at], 1, 1)
        if i == 0:
            mlp_out[...] = out
            grad_two[...] = back
        else:
            mlp_out[...] = mlp_out[...] + out
            grad_two[...] = grad_two[...] + back
        sum_up[:, at] = jnp.sum(grad.astype(F32).reshape(64, 8, part), axis=0)
        for pair in range(2):
            gup, gdown = [], []
            for k in (2 * pair, 2 * pair + 1):
                owner = pl.ds(pl.multiple_of(part * ids[k], part), part)
                gup.append(dot(two_t[owner, :], grad).reshape(2, 4, 4, 8, part))
                gdown.append(dot(cots_t[part * k : part * (k + 1), :], act).reshape(4, 8, 8, part))
            for n in range(4):
                piece = jnp.concatenate([v[:, :, n] for v in gup], axis=2).reshape(8, 16, part)
                by_z[n, :, pair, :, at] = piece.astype(BF16)
                piece = jnp.concatenate([v[n] for v in gdown], axis=1)
                (y0, y1, y2, y3)[n][:, pair, :, at] = piece.astype(BF16)


def finish_kernel(
    ids, back, w_all, dense, x0, x1, x2, x3, vec, cosine, sine_low, sine_high, one_t, cots, mlp_out, grad_two, sum_up,
    message, own_part, sent, sent_far, grads, att, g_one, sums, dense_grad,
    tokens, mlp_here, two_here, sems,
):
    rows, part = 128, 256
    late = [(x.at[0:rows, :], tokens.at[k]) for k, x in enumerate((x0, x1, x2, x3))]
    late += [(mlp_out, mlp_here), (grad_two, two_here)]
    late = [pltpu.make_async_copy(source, into, sems.at[n]) for n, (source, into) in enumerate(late)]
    for copy in late:
        copy.start()
    lane = lax.broadcasted_iota(jnp.int32, (rows, 128), 1)
    first = lane < HEAD_DIM
    for k in range(4):
        at = slice(k * rows, (k + 1) * rows)
        pieces = [[], [], [], []]
        for p in range(2):
            kvs, qas = [], []
            for odd in range(2):
                base = (4 * k + 2 * p + odd) * 2
                kvs.append(back[base, 0:128, :].astype(F32) + back[base + 1, 0:128, :].astype(F32))
                qas.append(
                    jnp.concatenate([back[base, 128:192, :].astype(F32), back[base + 1, 128:192, :].astype(F32)], axis=0)
                )
            for into, pair in ((pieces[1], kvs), (pieces[0], qas)):
                into.append(jnp.where(first, pair[0], pltpu.roll(pair[1], 64, 1)))
            for into, pair in ((pieces[2], kvs), (pieces[3], qas)):
                into.append(jnp.where(first, pltpu.roll(pair[0], 64, 1), pair[1]))
        dq, dk, dv, out = (jnp.concatenate(piece, axis=1) for piece in pieces)
        dq = turned(dq, cosine[...], -sine_low[...], -sine_high[...])
        dk = turned(dk, cosine[...], -sine_low[...], -sine_high[...])
        grads[at, 0:part] = dq.astype(BF16)
        grads[at, part : 2 * part] = dk.astype(BF16)
        grads[at, 2 * part :] = dv.astype(BF16)
        att[at, :] = out.astype(BF16)
    dense_grad[...] = dot(att[...], cots[...], 0, 0).reshape(32, 8, 4 * part)
    for k in range(4):
        owner = pl.ds(pl.multiple_of(part * ids[k], part), part)
        gqkv = dot(one_t[owner, :], grads[...]).reshape(32, 8, 3 * part)
        lower = jnp.concatenate([gqkv[:, :, 512:], dense_grad[:, :, owner]], axis=2)
        message[:, :, pl.ds(pl.multiple_of(512 * ids[k], 512), 512)] = jnp.concatenate([gqkv[:, :, :512], lower], axis=1).astype(BF16)
    g_one[...] = dot(grads[...], w_all[...], 1, 1)
    gone, gtwo = vec[0:1, :], vec[2:3, :]
    biases = vec[4:5, :] + vec[5:6, :]
    folded = [jnp.zeros((8, 4 * part), F32) for _ in range(5)]
    for copy in late:
        copy.wait()
    for k in range(4):
        at = slice(k * rows, (k + 1) * rows)
        normal, spread = normalise(tokens[k])
        one, two = g_one[at, :], two_here[at, :]
        cot = cots[at, :].astype(F32)
        for i, value in enumerate((one * normal, one, two * normal, two, cot)):
            folded[i] = folded[i] + jnp.sum(value.reshape(16, 8, 4 * part), axis=0)
        e = one * gone + two * gtwo
        inner = spread * (
            e - jnp.mean(e, axis=-1, keepdims=True) - normal * jnp.mean(e * normal, axis=-1, keepdims=True)
        )
        outer = mlp_here[at, :] + dot(att[at, :], dense[...])
        if k == 0:
            own_part[:, 0 : 4 * part] = outer + tokens[k].astype(F32) + biases
            own_part[:, 4 * part :] = inner + cot
        else:
            into = sent_far if k == 2 else sent.at[k // 2]
            into[:, 0 : 4 * part] = outer.astype(BF16)
            into[:, 4 * part :] = inner.astype(BF16)
    row = lax.broadcasted_iota(jnp.int32, (16, 128), 0)

    def put(v, values):
        block = jnp.zeros((16, 128), F32)
        for k, value in enumerate(values):
            block = jnp.where(row == 4 * ids[k], value[:, 0:128], block)
            block = jnp.where(row == 4 * ids[k] + 1, value[:, 128:256], block)
        message[v, :, 2048:2176] = block.astype(BF16)

    sums[...] = jnp.zeros_like(sums)
    for i in range(5):
        sums[i : i + 1, :] = jnp.sum(folded[i], axis=0, keepdims=True)
    message[:, :, 2048:2176] = jnp.zeros((32, 16, 128), BF16)
    total = jnp.sum(grads[...].astype(F32), axis=0, keepdims=True)
    ups = jnp.sum(sum_up[...], axis=0, keepdims=True)
    owners = [pl.ds(pl.multiple_of(part * ids[k], part), part) for k in range(4)]
    for v in range(4):
        put(v, [sums[v : v + 1, owner] for owner in owners])
    for v in range(3):
        put(4 + v, [total[:, part * v : part * (v + 1)]] * 4)
    put(7, [sums[4:5, owner] for owner in owners])
    for v in range(4):
        put(8 + v, [ups[:, part * v : part * (v + 1)]] * 4)


def place_kernel(
    ids, u0, u1, u2, v2, u3, d0, d1, d2, e2, d3, tail, up, down, qkv, dense,
    up_rows, down_rows, qkv_rows, dense_rows, sems,
):
    width = 2048
    copies = []

    def send(rows, out, n):
        copies.append(pltpu.make_async_copy(rows, out, sems.at[n]))
        copies[-1].start()

    def put(piece, into):
        value = piece.astype(F32)
        into[:, 0:width] = value[0:8, :]
        into[:, width:] = value[8:16, :]

    for d, (one, two) in enumerate(((u0, d0), (u1, d1), (u3, d3), ((u2, v2), (d2, e2)))):
        steps = (0, 1, 3, 2)[d]
        for e in range(4):
            near_y, near_z = lax.rem(ids[0] + 4 - e, 4), lax.rem(ids[1] + 4 - e, 4)
            for x in range(2):
                if steps == 2:
                    piece_one, piece_two = one[e // 2][e % 2, x], two[e // 2][e % 2, x]
                else:
                    piece_one, piece_two = one[e, x], two[e, x]
                put(piece_one, up_rows.at[d, 4 * x + near_y])
                put(piece_two, down_rows.at[d, x, near_z])
        send(up_rows.at[d], up.at[:, lax.rem(ids[1] + 4 - steps, 4)], 2 * d)
        send(down_rows.at[d], down.at[:, lax.rem(ids[0] + 4 - steps, 4)], 2 * d + 1)
    qkv_rows[...] = tail[:, 0:3072].astype(F32)
    send(qkv_rows, qkv, 8)
    dense_rows[...] = tail[:, 3072:4096].astype(F32)
    send(dense_rows, dense, 9)
    for copy in copies:
        copy.wait()


def local(kernel, ids, inputs, outs, scratch, limit, micros, space=pltpu.VMEM, late=()):
    shapes = [jax.ShapeDtypeStruct(shape, dtype) for shape, dtype in outs]
    moved = sum(v.size * v.dtype.itemsize for v in list(inputs) + shapes)
    return pl.pallas_call(
        kernel,
        grid_spec=pltpu.PrefetchScalarGridSpec(
            num_scalar_prefetch=1,
            grid=(),
            in_specs=[
                pl.BlockSpec(memory_space=pl.ANY if n in late else pltpu.VMEM) for n in range(len(inputs))
            ],
            out_specs=[pl.BlockSpec(memory_space=space)] * len(outs),
            scratch_shapes=[pltpu.VMEM(*item) if item else pltpu.SemaphoreType.DMA((10,)) for item in scratch],
        ),
        out_shape=shapes,
        compiler_params=pltpu.CompilerParams(vmem_limit_bytes=limit * 1024 * 1024),
        cost_estimate=pl.CostEstimate(flops=micros * 10**9, bytes_accessed=moved, transcendentals=0),
    )(ids, *inputs)


def swap(value, flip):
    return lax.ppermute(value, "fsdp", [(i, i ^ flip) for i in range(4)])


def across(value, flip_ctx, flip):
    order = [(4 * c + f, 4 * (c ^ flip_ctx) + (f ^ flip)) for c in range(32) for f in range(4)]
    return lax.ppermute(value, ("ctx", "fsdp"), order)


def along(value, steps_y, steps_z):
    order = []
    for c in range(32):
        x, y, z = c // 16, (c // 4) % 4, c % 4
        order.append((c, 16 * x + 4 * ((y + steps_y) % 4) + (z + steps_z) % 4))
    return lax.ppermute(value, "ctx", order)


def flipped(value, flip):
    return lax.ppermute(value, "ctx", [(c, c ^ flip) for c in range(32)])


def beside(far):
    both = jnp.concatenate(far)
    return [along(both, 1, 0), along(both, 0, 1), along(both, -1, -1)]


def on_device(
    tokens,
    block_order,
    weight_qkv,
    bias_qkv,
    weight_dense,
    bias_dense,
    weight_up,
    bias_up,
    weight_down,
    bias_down,
    gain_one,
    shift_one,
    gain_two,
    shift_two,
    cotangent,
):
    rows = tokens.shape[2]
    width = tokens.shape[3]
    blocks = lax.axis_size("ctx")
    ctx = lax.axis_index("ctx").astype(jnp.int32)
    mine = lax.axis_index("fsdp").astype(jnp.int32)
    part = width // 4
    at_x, at_y, at_z = ctx // 16, (ctx // 4) % 4, ctx % 4
    quarter = 2 * (at_y % 2) + at_z % 2
    ids = jnp.stack([mine, mine ^ 1, mine ^ 2, mine ^ 3, quarter] + [(n - at_y) % 4 for n in range(4)] + [quarter ^ 2, quarter ^ 1, quarter ^ 3])
    own_tokens = tokens.reshape(rows, width)
    own_cot = cotangent.reshape(rows, width)

    def gather(value):
        over = swap(value, 2)
        return [value, swap(value, 1), over, swap(over, 1)]

    packed, qkv_own, qkv_core, *qkv_far = local(
        start_kernel,
        ids,
        [
            own_tokens, own_cot, weight_qkv,
            gain_one, shift_one, gain_two, shift_two, bias_dense, bias_down, bias_qkv,
        ],
        [((272, width), BF16), ((part, 768), BF16), ((part, 768), BF16), ((64, 768), BF16), ((64, 768), BF16)],
        [],
        60,
        4,
    )
    feed_own, feed_core, *feed_far = local(
        feed_start_kernel,
        ids,
        [weight_up, weight_down],
        [((part, 2 * width), BF16)] * 2 + [((64, 2 * width), BF16)] * 2,
        [],
        60,
        5,
    )
    qkv_far = [across(piece, 16, k) for k, piece in zip((2, 3), qkv_far)]
    packed = gather(packed)
    feed_far, qkv_far, packed[2] = lax.optimization_barrier((feed_far, qkv_far, packed[2]))
    qkv_pieces = [qkv_own, swap(qkv_core, 1), *qkv_far, *beside(qkv_far)]
    feed_far = [across(piece, 16, k) for k, piece in zip((2, 3), feed_far)]
    feed_core = swap(feed_core, 1)

    places = (block_order[ctx] * rows + lax.broadcasted_iota(jnp.int32, (rows, part), 0)).astype(F32)
    lane = lax.broadcasted_iota(jnp.int32, (rows, part), 1) % HEAD_DIM
    halfway = ROT_DIMS // 2
    inverse = 10000.0 ** (-2.0 * (lane % halfway).astype(F32) / ROT_DIMS)
    phases = jnp.where(lane < ROT_DIMS, places * inverse, 0.0)
    sines = jnp.sin(phases)
    tables = [
        jnp.cos(phases),
        jnp.where(lane < halfway, -sines, 0.0),
        jnp.where(lane < halfway, 0.0, sines),
    ]

    message, low_one, low_two, four_cot, my_qkv, vec = local(
        prepare_kernel,
        ids,
        [*packed, *qkv_pieces, weight_dense, *tables],
        [
            ((blocks, 192, 128), BF16),
            ((4 * rows, width), BF16),
            ((4 * rows, width), BF16),
            ((4 * rows, width), BF16),
            ((width, 3 * part), BF16),
            ((8, width), F32),
        ],
        [((1, 3 * width), F32), ((4 * rows, 3 * part), F32), ((4 * rows, part), F32)],
        60,
        7,
    )
    message, feed_far = lax.optimization_barrier((message, feed_far))
    feed_pieces = [feed_own, feed_core, *feed_far, *beside(feed_far)]
    message, feed_pieces = lax.optimization_barrier((message, feed_pieces))
    received = lax.all_to_all(message, "ctx", 0, 0, tiled=True)
    order = jnp.zeros((blocks,), jnp.int32).at[block_order].set(jnp.arange(blocks, dtype=jnp.int32))
    order = jnp.concatenate([order, (ctx % 2)[None]])

    by_z, y0, y1, y2, y3, mlp_out, grad_two, sum_up, one_t = local(
        feed_kernel,
        ids,
        [low_one, low_two, four_cot, *feed_pieces, bias_up.astype(F32).reshape(1, width)],
        [
            ((4, 8, 2, 16, width), BF16),
            ((8, 2, 16, width), BF16),
            ((8, 2, 16, width), BF16),
            ((8, 2, 16, width), BF16),
            ((8, 2, 16, width), BF16),
            ((4 * rows, width), F32),
            ((4 * rows, width), F32),
            ((8, width), F32),
            ((width, 4 * rows), BF16),
        ],
        [((width, width), BF16), ((width, width), BF16), ((width, 4 * rows), BF16), ((width, 4 * rows), BF16)],
        60,
        14,
    )
    natural = jnp.arange(4) ^ mine

    def spread(chunk):
        copies = jnp.broadcast_to(chunk[None], (blocks,) + chunk.shape)
        return lax.all_to_all(copies, "ctx", 0, 0, tiled=True).reshape(blocks * chunk.shape[0], chunk.shape[1])

    def added(pieces):
        total = pieces[0].astype(F32)
        for piece in pieces[1:]:
            total = total + piece.astype(F32)
        return total.astype(BF16)

    def pick(value, axis, n):
        return lax.dynamic_index_in_dim(value, n, axis, keepdims=False)

    groups = [[4 * n + z for z in range(4)] for n in range(8)]
    up_in = lax.all_to_all(by_z, "ctx", 0, 0, tiled=True, axis_index_groups=groups)
    down_in = [y0] + [along(y, d + 1, 0) for d, y in enumerate((y1, y2, y3))]
    answer = attention(order, received)
    answer, up_in, down_in = lax.optimization_barrier((answer, up_in, down_in))
    up_sum = added([up_in[n] for n in range(4)]).reshape(2, 4, 2, 16, width)
    down_sum = added(down_in).reshape(2, 4, 2, 16, width)

    up_in = [pick(up_sum, 1, at_y)] + [along(pick(up_sum, 1, (at_y + d) % 4), d, 0) for d in range(1, 4)]
    down_in = [pick(down_sum, 1, at_z)] + [along(pick(down_sum, 1, (at_z + d) % 4), 0, d) for d in range(1, 4)]
    back = lax.all_to_all(answer, "ctx", 0, 0, tiled=True)
    back, up_in, down_in = lax.optimization_barrier((back, up_in, down_in))
    feed_sum = jnp.stack([added(up_in), added(down_in)], axis=1)
    feed_slots = feed_sum.reshape(2, 2, 4, 8, width)
    feed_cross = [feed_slots[:, :, 0]] + [swap(feed_slots[:, :, k], k) for k in range(1, 4)]
    feed_cross = jnp.stack(feed_cross)[natural]

    tail, own_part, sent, sent_far = local(
        finish_kernel,
        ids,
        [back, my_qkv, weight_dense, *packed, vec, *tables, one_t, four_cot, mlp_out, grad_two, sum_up],
        [((blocks, 16, 2176), BF16), ((rows, 2 * width), F32), ((2, rows, 2 * width), BF16), ((rows, 2 * width), BF16)],
        [((4 * rows, 3 * part), BF16), ((4 * rows, part), BF16), ((4 * rows, width), F32), ((8, width), F32), ((32, 8, width), F32),
         ((4, rows, width), BF16), ((4 * rows, width), F32), ((4 * rows, width), F32), None],
        60,
        12,
        late=(3, 4, 5, 6, 13, 14),
    )
    tail, feed_cross = lax.optimization_barrier((tail, feed_cross))
    feed_pair = added([feed_cross, across(feed_cross, 16, 0)]).reshape(2, 2, 2, 2, 8, width)
    feed_pair = feed_pair.transpose(3, 2, 0, 4, 1, 5).reshape(2, 2, 16, 2 * width)
    tail_arrived = lax.all_to_all(tail, "ctx", 0, 0, tiled=True)

    near = swap(sent, 1).astype(F32)
    both = own_part + near[0] + swap((sent_far.astype(F32) + near[1]).astype(BF16), 2).astype(F32)
    out_block, grad_tokens = both[:, :width].astype(BF16), both[:, width:].astype(BF16)

    up_four = jnp.stack([feed_pair[0]] + [along(feed_pair[0], d, 0) for d in range(1, 4)])
    down_four = jnp.stack([feed_pair[1]] + [along(feed_pair[1], 0, d) for d in range(1, 4)])
    tail_arrived, up_four, down_four, out_block, grad_tokens = lax.optimization_barrier(
        (tail_arrived, up_four, down_four, out_block, grad_tokens)
    )
    up_one, up_three = along(up_four, 0, 1), along(up_four, 0, 3)
    down_one, down_three = along(down_four, 1, 0), along(down_four, 3, 0)
    summed = jnp.sum(tail_arrived.astype(F32), axis=0).astype(BF16)
    slots = summed[:, : 2 * width].reshape(16, 4, 512).transpose(1, 0, 2)
    small = summed[:, 2 * width :].reshape(4, 4, 128)
    crossed = jnp.concatenate([slots, jnp.pad(small, ((0, 0), (0, 12), (0, 0)))], axis=2)
    crossed = lax.all_to_all(crossed, "fsdp", 0, 0, tiled=True)
    mat_qkv = jnp.concatenate([crossed[:, :8, :512], crossed[:, 8:, :part]], axis=2)
    mat_qkv = mat_qkv.reshape(4, 8, 3, part).transpose(1, 2, 0, 3).reshape(8, 3 * width)
    mat_dense = slots[:, 8:, part:].transpose(1, 0, 2).reshape(8, width)
    near = crossed[:, :2, 512:].reshape(4, part)
    vector = jnp.concatenate(
        [
            near.reshape(width),
            jnp.sum(near.astype(F32), axis=0).astype(BF16),
            pick(small, 0, mine)[:2].reshape(part),
            jnp.zeros((2 * part,), BF16),
        ]
    ).reshape(8, part)
    chunk = jnp.concatenate([mat_qkv, mat_dense, vector], axis=1)
    chunk, up_one, up_three, down_one, down_three = lax.optimization_barrier(
        (chunk, up_one, up_three, down_one, down_three)
    )
    tail_full = spread(chunk)
    up_all = [up_four, up_one, along(up_one[:2], 0, 1), along(up_three[2:], 0, 3), up_three]
    down_all = [down_four, down_one, along(down_one[:2], 1, 0), along(down_three[2:], 3, 0), down_three]

    g_up, g_down, g_qkv, g_dense = local(
        place_kernel,
        jnp.stack([at_y, at_z]),
        [*up_all, *down_all, tail_full],
        [((8, 4, 8, 4 * width), F32), ((2, 4, 4, 8, 4 * width), F32), ((part, 3 * width), F32), ((part, width), F32)],
        [
            ((4, 8, 8, 4 * width), F32),
            ((4, 2, 4, 8, 4 * width), F32),
            ((part, 3 * width), F32),
            ((part, width), F32),
            None,
        ],
        60,
        6,
        pl.ANY,
    )
    g_up, g_down = g_up.reshape(part, 4 * width), g_down.reshape(part, 4 * width)
    vector = tail_full[:, 4 * width :].reshape(blocks, 2 * width).astype(F32)
    g_bqkv = lax.dynamic_slice_in_dim(vector[4:7, :width].reshape(3 * width), mine * 768, 768)
    g_norm = vector[:4, width : width + part]
    g_cot = vector[7, width + part : width + 2 * part]
    g_bup = vector[8:12, width + part : width + 2 * part].reshape(width)
    return (
        out_block.reshape(tokens.shape),
        grad_tokens.reshape(tokens.shape),
        g_qkv,
        g_bqkv,
        g_dense,
        g_cot,
        g_up,
        g_bup,
        g_down,
        g_cot,
        g_norm[0],
        g_norm[1],
        g_norm[2],
        g_norm[3],
    )


def solution(mesh):
    block = P("ctx", "fsdp", None, None)
    matrix = P("fsdp", None)
    vector = P("fsdp")
    return jax.shard_map(
        on_device,
        mesh=mesh,
        in_specs=(
            block,
            P(),
            matrix,
            vector,
            matrix,
            vector,
            matrix,
            vector,
            matrix,
            vector,
            vector,
            vector,
            vector,
            vector,
            block,
        ),
        out_specs=(
            block,
            block,
            matrix,
            vector,
            matrix,
            vector,
            matrix,
            vector,
            matrix,
            vector,
            vector,
            vector,
            vector,
            vector,
        ),
        check_vma=False,
    )
```
